32 devices in a mesh: rows: 32 (over z, y, x, core).
Axes of the slice: x: 2, y: 2, z: 4, core: 2. Of those that a mesh axis runs over, the one named last changes fastest.
Arguments:
- residual: float32 [16384, 128], P('rows'), may hold values from -6 to 6
- inv_diag: float32 [16384, 512], P('rows'), may hold values from -0.25 to 0.25
- coupling_tiles: float32 [16384, 6, 512], P('rows'), may hold values from -0.0546875 to 0.0546875
- colour: int32 [32], P('rows'), may hold values from 0 to 3, as said below
- tile_cols: int32 [32, 6], P('rows'), may hold values from 0 to 31, as said below
Outputs:
- precond: float32 [16384, 128], P('rows')
The draws below stay inside these ranges and needn't reach their ends.
Inputs may be any that keep to these rules, and one draw needn't show every extreme that they name: Every aligned group of 4 blocks (blocks 4 g to 4 g + 3) holds each colour exactly once. `tile_cols`: row b lists 6 distinct blocks, each within 4 places of b along the cycle of blocks (indices modulo 32), none equal to b and none of b's colour.
All inputs are finite; a program needn't handle non-finite values.
Results may differ from the reference program's by a relative error of at most 0.0001.
Values sent between devices are 32-bit elements; how exact they have to be, the bound alone decides.
No kernel may reach another device: no remote copies, remote signals or barrier semaphores. Data moves between devices by JAX's collectives and lax.ppermute only.
A program may use at most 128 MiB of HBM per device.

```python
import jax
import jax.numpy as jnp
from jax import lax

BLOCK = 512
COLS = 128
TILES = 6
COLOURS = 4
REACH = 4
NBLK = 32
NODES = 16384


def colour_and_tiles(key):
    base_key = jax.random.fold_in(key, 11)
    group_keys = jax.random.split(jax.random.fold_in(base_key, 1), NBLK // COLOURS)
    colours = jax.vmap(lambda subkey: jax.random.permutation(subkey, COLOURS))(group_keys).reshape(NBLK).astype(jnp.int32)
    offset_table = jnp.concatenate([jnp.arange(-REACH, 0), jnp.arange(1, REACH + 1)]).astype(jnp.int32)
    blocks = jnp.arange(NBLK, dtype=jnp.int32)
    candidates = (blocks[:, None] + offset_table[None, :]) % NBLK
    same_colour = (colours[candidates] == colours[:, None]).astype(jnp.int32)
    order_keys = jax.random.split(jax.random.fold_in(base_key, 2), NBLK)
    shuffle = jax.vmap(lambda subkey: jax.random.permutation(subkey, 2 * REACH))(order_keys).astype(jnp.int32)
    scores = shuffle + 2 * REACH * same_colour
    picked = jax.lax.top_k(-scores, TILES)[1]
    chosen = jnp.take_along_axis(candidates, picked, axis=1)
    return (colours, chosen.astype(jnp.int32))


def draw_colour(key, part):
    return colour_and_tiles(key)[0]


def draw_tile_cols(key, part):
    return colour_and_tiles(key)[1]


def block_scale(key, extent, pieces, smallest, top_value):
    level, own = 1.0, jax.random.fold_in(key, 6)
    for dim, shards_of in pieces:
        heights = jnp.exp(jax.random.uniform(jax.random.fold_in(own, dim), (shards_of,), jnp.float32, smallest / len(pieces), top_value / len(pieces)))
        level = level * jnp.repeat(heights, extent[dim] // shards_of).reshape([-1 if axis == dim else 1 for axis in range(len(extent))])
    return level


def noise(key, dims, deviation, limit, pieces=(), kind=jnp.bfloat16):
    level = block_scale(key, dims, pieces, -0.22, 0.18) if pieces else 1.0
    array = jax.random.normal(key, dims, jnp.float32) * deviation * level
    return jnp.minimum(jnp.maximum(array, -limit), limit).astype(kind)


def setup_inputs(seed: int = 0) -> dict:
    keys = jax.random.split(jax.random.key(seed), 6)
    return {
        "residual": noise(keys[0], (NODES, COLS), 1.0, 6.0, ((0, 32),), jnp.float32),
        "inv_diag": noise(keys[1], (NODES, BLOCK), BLOCK ** -0.5, 0.25, ((0, 32),), jnp.float32),
        "coupling_tiles": noise(keys[2], (NODES, TILES, BLOCK), (4 * TILES * BLOCK) ** -0.5, 0.0546875, ((0, 32),), jnp.float32),
        "colour": draw_colour(jax.random.fold_in(keys[5], 71), 0),
        "tile_cols": draw_tile_cols(jax.random.fold_in(keys[5], 71), 0),
    }


def relax_colour(current, colour_now, residual, inv_diag, coupling_tiles, colour, tile_cols):
    blocks_x = current.reshape(NBLK, BLOCK, COLS)
    active = jnp.nonzero(colour == colour_now, size=NBLK // COLOURS)[0].astype(jnp.int32)

    def single(block_id):
        first_row = block_id * BLOCK
        couple = lax.dynamic_slice_in_dim(coupling_tiles, first_row, BLOCK, 0).reshape(BLOCK, TILES * BLOCK)
        neighbours = blocks_x[tile_cols[block_id]].reshape(TILES * BLOCK, COLS)
        coupled = jnp.dot(couple, neighbours, precision=lax.Precision.HIGHEST)
        inverse = lax.dynamic_slice_in_dim(inv_diag, first_row, BLOCK, 0)
        rhs_block = lax.dynamic_slice_in_dim(residual, first_row, BLOCK, 0)
        return jnp.dot(inverse, rhs_block - coupled, precision=lax.Precision.HIGHEST)

    updated = lax.map(single, active)
    return blocks_x.at[active].set(updated).reshape(NBLK * BLOCK, COLS)


def reference(residual, inv_diag, coupling_tiles, colour, tile_cols):
    current = jnp.zeros(residual.shape, jnp.float32)
    sweep_order = list(range(COLOURS)) + list(range(COLOURS - 1, -1, -1))
    for colour_now in sweep_order:
        current = relax_colour(current, colour_now, residual, inv_diag, coupling_tiles, colour, tile_cols)
    return current
```

```python
import functools

import jax
import jax.numpy as jnp
from jax import lax
from jax.experimental import pallas as pl
from jax.experimental.pallas import tpu as pltpu
from jax.sharding import PartitionSpec as P

COLOURS = 4
SIDES = 3
OWN_COLOUR = 0
SIB_COLOUR = 1
TILE_START = 2
VMEM_LIMIT = 56 * 1024 * 1024


def dot(a, b):
    return jnp.dot(a, b, preferred_element_type=jnp.float32)


def split(value):
    high = value.astype(jnp.bfloat16).astype(jnp.float32)
    return high, value - high


def left_lanes(shape):
    return lax.broadcasted_iota(jnp.int32, shape, 1) < shape[1] // 2


def swap_halves(value):
    return pltpu.roll(value, value.shape[1] // 2, 1)


def both_parts(packed):
    high, low = split(packed)
    left = left_lanes(packed.shape)
    upper = jnp.where(left, high, swap_halves(low))
    lower = jnp.where(left, swap_halves(high), low)
    return jnp.concatenate([upper, lower], axis=0).astype(jnp.bfloat16)


def vmem():
    return pl.BlockSpec(memory_space=pltpu.VMEM)


def smem():
    return pl.BlockSpec(memory_space=pltpu.SMEM)


def anywhere():
    return pl.BlockSpec(memory_space=pl.ANY)


def params():
    return pltpu.CompilerParams(vmem_limit_bytes=VMEM_LIMIT)


def first_kernel(core_ref, inverse_ref, residual_ref, keep_ref, send_ref):
    d_high, d_low = split(inverse_ref[...])
    r_high, r_low = split(residual_ref[...])
    d_high, d_low, r_high, r_low = (v.astype(jnp.bfloat16) for v in (d_high, d_low, r_high, r_low))
    value = dot(d_high, r_high) + (dot(d_high, r_low) + dot(d_low, r_high))
    half = value.shape[0] // 2
    upper, lower = value[:half], value[half:]
    left = left_lanes(upper.shape)
    first = jnp.where(left, upper, swap_halves(lower))
    second = jnp.where(left, swap_halves(upper), lower)
    is_first = core_ref[0] == 0
    keep_ref[...] = jnp.where(is_first, first, second)
    send_ref[...] = jnp.where(is_first, second, first)


def last_kernel(core_ref, mine_ref, other_ref, out_ref):
    is_first = core_ref[0] == 0
    mine, other = mine_ref[...], other_ref[...]
    first = jnp.where(is_first, mine, other)
    second = jnp.where(is_first, other, mine)
    half = mine.shape[0]
    left = left_lanes(mine.shape)
    out_ref[:half] = jnp.where(left, first, swap_halves(second))
    out_ref[half:] = jnp.where(left, swap_halves(first), second)


def tile_of(meta_ref, own, tiles, colour, side):
    wanted = meta_ref[TILE_START + 2 * tiles + side * COLOURS + colour]
    start = jnp.where(own, TILE_START, TILE_START + tiles)
    found = jnp.int32(-1)
    for k in range(tiles):
        found = jnp.where(meta_ref[start + k] == wanted, k, found)
    return found


def gather_kernel(now, newest, older, meta_ref, own_tiles, sib_tiles, own_inverse, sib_inverse, *refs):
    known = refs[: SIDES * len(older)]
    w_high, w_low, d_high, d_low, partial = refs[SIDES * len(older) : SIDES * len(older) + 5]
    buffer, total, sems = refs[SIDES * len(older) + 5 :]
    tiles, block = own_tiles.shape[0], own_tiles.shape[1]
    own = meta_ref[OWN_COLOUR] == now
    active = own | (meta_ref[SIB_COLOUR] == now)
    slots = [(newest, side) for side in range(SIDES)] + [(c, side) for c in older for side in range(SIDES)]

    @pl.when(active)
    def _():
        def fetch(own_src, sib_src, slot, start):
            @pl.when(own)
            def _():
                copy = pltpu.make_async_copy(own_src, buffer.at[slot], sems.at[slot])
                copy.start() if start else copy.wait()

            @pl.when(jnp.logical_not(own))
            def _():
                copy = pltpu.make_async_copy(sib_src, buffer.at[slot], sems.at[slot])
                copy.start() if start else copy.wait()

        which = [tile_of(meta_ref, own, tiles, c, side) for c, side in slots]
        fetch(own_inverse, sib_inverse, len(slots), True)
        for slot, k in enumerate(which):
            @pl.when(k >= 0)
            def _():
                fetch(own_tiles.at[k], sib_tiles.at[k], slot, True)

        fetch(own_inverse, sib_inverse, len(slots), False)
        high, low = split(buffer[len(slots)])
        d_high[...] = high.astype(jnp.bfloat16)
        d_low[...] = low.astype(jnp.bfloat16)
        total[...] = jnp.zeros_like(total)
        for slot, k in enumerate(which):
            span = pl.ds(slot * block, block)

            @pl.when(k >= 0)
            def _():
                fetch(own_tiles.at[k], sib_tiles.at[k], slot, False)
                high, low = split(buffer[slot])
                high, low = high.astype(jnp.bfloat16), low.astype(jnp.bfloat16)
                if slot < SIDES:
                    w_high[:, span] = high
                    w_low[:, span] = low
                else:
                    value = both_parts(known[slot - SIDES][...])
                    total[...] += dot(high, value) + dot(low, value)

            if slot < SIDES:
                @pl.when(k < 0)
                def _():
                    w_high[:, span] = jnp.zeros((block, block), jnp.bfloat16)
                    w_low[:, span] = jnp.zeros((block, block), jnp.bfloat16)

        partial[...] = total[...] + swap_halves(total[...])


def relax_kernel(now, meta_ref, w_high, w_low, d_high, d_low, partial, behind, here, ahead, own_start, sib_start, out_ref, stacked):
    own = meta_ref[OWN_COLOUR] == now
    active = own | (meta_ref[SIB_COLOUR] == now)
    block = d_high.shape[0]

    @pl.when(active)
    def _():
        for side, ref in enumerate((behind, here, ahead)):
            stacked[pl.ds(side * block, block), :] = both_parts(ref[...])
        value = stacked[...]
        coupled = dot(w_high[...], value) + dot(w_low[...], value)
        coupled = partial[...] + (coupled + swap_halves(coupled))
        high, low = split(coupled)
        operand = jnp.where(left_lanes(high.shape), high, low).astype(jnp.bfloat16)
        change = dot(d_high[...], operand) + dot(d_low[...], operand)
        change = change + swap_halves(change)
        upper, lower = change[: block // 2], change[block // 2 :]
        start = jnp.where(own, own_start[...], sib_start[...])
        out_ref[...] = start - jnp.where(left_lanes(upper.shape), upper, lower)


def gather(now, newest, older, meta, own_tiles, sib_tiles, own_inverse, sib_inverse, known):
    block, cols = own_tiles.shape[1], known[newest][0].shape[1]
    slots = SIDES * (1 + len(older)) + 1
    operands = [value for c in older for value in known[c]]
    return pl.pallas_call(
        functools.partial(gather_kernel, now, newest, older),
        out_shape=[
            pltpu.VMEM((block, SIDES * block), jnp.bfloat16),
            pltpu.VMEM((block, SIDES * block), jnp.bfloat16),
            pltpu.VMEM((block, block), jnp.bfloat16),
            pltpu.VMEM((block, block), jnp.bfloat16),
            pltpu.VMEM((block, cols), jnp.float32),
        ],
        in_specs=[smem()] + [anywhere()] * 4 + [vmem()] * len(operands),
        out_specs=[vmem()] * 5,
        scratch_shapes=[
            pltpu.VMEM((slots, block, block), jnp.float32),
            pltpu.VMEM((block, cols), jnp.float32),
            pltpu.SemaphoreType.DMA((slots,)),
        ],
        compiler_params=params(),
        cost_estimate=pl.CostEstimate(
            flops=4 * block * block * cols * slots, bytes_accessed=4 * block * block * slots, transcendentals=0
        ),
        name=f"gather_{now}_{newest}",
    )(meta, own_tiles, sib_tiles, own_inverse, sib_inverse, *operands)


def relax(now, meta, gathered, latest, own_start, sib_start):
    block, cols = gathered[2].shape[0], own_start.shape[1]
    gathered = [pltpu.with_memory_space_constraint(g, pltpu.VMEM) for g in gathered]
    return pl.pallas_call(
        functools.partial(relax_kernel, now),
        out_shape=jax.ShapeDtypeStruct(own_start.shape, jnp.float32),
        in_specs=[smem()] + [vmem()] * 10,
        out_specs=vmem(),
        scratch_shapes=[pltpu.VMEM((SIDES * block, cols), jnp.bfloat16)],
        compiler_params=params(),
        cost_estimate=pl.CostEstimate(
            flops=16 * block * block * cols, bytes_accessed=16 * block * block, transcendentals=0
        ),
        name=f"relax_{now}",
    )(meta, *gathered, *latest, own_start, sib_start)


def per_device(residual, inv_diag, coupling_tiles, colour, tile_cols):
    axis = "rows"
    count = lax.axis_size(axis)
    groups = count // COLOURS
    me = lax.axis_index(axis)
    core = (me % 2).reshape(1)
    place = me % COLOURS
    group = me // COLOURS
    block, cols = residual.shape
    tiles = jnp.transpose(coupling_tiles, (1, 0, 2))
    number = tiles.shape[0]

    def flip(value, bit):
        return lax.ppermute(value, axis, [(i, i ^ bit) for i in range(count)])

    def shift(value, by):
        return lax.ppermute(value, axis, [(i, (i + by) % count) for i in range(count)])

    own_facts = jnp.concatenate([colour, tile_cols[0]])
    sib_facts = flip(own_facts, 1)
    own_colour, sib_colour = own_facts[0], sib_facts[0]
    wheel = jnp.arange(COLOURS, dtype=jnp.int32)
    pair_places = jnp.where(wheel == own_colour, place, 0) + jnp.where(wheel == sib_colour, place ^ 1, 0)
    group_places = pair_places + flip(pair_places, 2)
    places = [shift(group_places, COLOURS), group_places, shift(group_places, -COLOURS)]
    blocks = [(((group + side - 1) % groups) * COLOURS + places[side]).astype(jnp.int32) for side in range(SIDES)]
    meta = jnp.concatenate([own_facts[:1], sib_facts[:1], own_facts[1:], sib_facts[1:]] + blocks)

    keep, send = pl.pallas_call(
        first_kernel,
        out_shape=[jax.ShapeDtypeStruct((block // 2, cols), jnp.float32)] * 2,
        in_specs=[smem(), vmem(), vmem()],
        out_specs=[vmem()] * 2,
        compiler_params=params(),
        name="first",
    )(core, inv_diag, residual)
    own_start, sib_start = keep, flip(send, 1)
    sib_inverse = flip(inv_diag, 1)
    sib_tiles = flip(tiles, 1)

    def spread(candidate, now):
        here_now = (own_colour == now) | (sib_colour == now)
        here = jnp.where(here_now, candidate, flip(candidate, 2))
        return [shift(here, COLOURS), here, shift(here, -COLOURS)]

    candidate = jnp.where(own_colour == 0, own_start, sib_start)
    own_final, sib_final = own_start, sib_start
    known = {0: spread(candidate, 0)}
    order = list(range(1, COLOURS)) + list(range(COLOURS - 2, -1, -1))
    newest = 0
    for step, now in enumerate(order):
        older = tuple(c for c in sorted(known) if c not in (now, newest))
        gathered = gather(now, newest, older, meta, tiles, sib_tiles, inv_diag, sib_inverse, known)
        candidate = relax(now, meta, gathered, known[newest], own_start, sib_start)
        if step >= COLOURS - 2:
            own_final = jnp.where(own_colour == now, candidate, own_final)
            sib_final = jnp.where(sib_colour == now, candidate, sib_final)
        if step < len(order) - 1:
            known[now] = spread(candidate, now)
        newest = now

    return pl.pallas_call(
        last_kernel,
        out_shape=jax.ShapeDtypeStruct((block, cols), jnp.float32),
        in_specs=[smem(), vmem(), vmem()],
        out_specs=vmem(),
        compiler_params=params(),
        name="last",
    )(core, own_final, flip(sib_final, 1))


def solution(mesh):
    in_specs = (P("rows", None), P("rows", None), P("rows", None, None), P("rows"), P("rows", None))
    out_specs = P("rows", None)
    return jax.shard_map(
        per_device, mesh=mesh, in_specs=in_specs, out_specs=out_specs, check_vma=False
    )
```

```python
import functools

import jax
import jax.numpy as jnp
from jax import lax
from jax.experimental import pallas as pl
from jax.experimental.pallas import tpu as pltpu
from jax.sharding import PartitionSpec as P

COLOURS = 4
SIDES = 3
CHAINS = 2
OWN_COLOUR = 0
SIB_COLOUR = 1
TILE_START = 2
VMEM_LIMIT = 48 * 1024 * 1024


def dot_t(a, b):
    return lax.dot_general(a, b, (((1,), (1,)), ((), ())), preferred_element_type=jnp.float32)


def split(value):
    high = value.astype(jnp.bfloat16)
    return high, (value - high.astype(jnp.float32)).astype(jnp.bfloat16)


def times(value, high, low):
    rows = value.shape[0]
    parts = jnp.concatenate(split(value), axis=0)
    product = dot_t(parts, high) + dot_t(parts, low)
    return product[:rows] + product[rows:]


def vmem():
    return pl.BlockSpec(memory_space=pltpu.VMEM)


def smem():
    return pl.BlockSpec(memory_space=pltpu.SMEM)


def anywhere():
    return pl.BlockSpec(memory_space=pl.ANY)


def params():
    return pltpu.CompilerParams(vmem_limit_bytes=VMEM_LIMIT)


def near(values):
    return [pltpu.with_memory_space_constraint(v, pltpu.VMEM) for v in values]


def first_kernel(core_ref, inverse_ref, residual_ref, keep_ref, send_ref):
    value = times(jnp.transpose(residual_ref[...]), *split(inverse_ref[...]))
    half = value.shape[0] // 2
    is_first = core_ref[0] == 0
    keep_ref[...] = jnp.where(is_first, value[:half], value[half:])
    send_ref[...] = jnp.where(is_first, value[half:], value[:half])


def last_kernel(core_ref, mine_ref, other_ref, out_ref):
    is_first = core_ref[0] == 0
    mine, other = mine_ref[...], other_ref[...]
    first = jnp.where(is_first, mine, other)
    second = jnp.where(is_first, other, mine)
    out_ref[...] = jnp.transpose(jnp.concatenate([first, second], axis=0))


def tile_of(meta_ref, own, tiles, colour, side):
    wanted = meta_ref[TILE_START + 2 * tiles + side * COLOURS + colour]
    start = jnp.where(own, TILE_START, TILE_START + tiles)
    found = jnp.int32(-1)
    for k in range(tiles):
        found = jnp.where(meta_ref[start + k] == wanted, k, found)
    return found


def gather_kernel(now, newest, older, has_base, n_after, meta_ref, own_tiles, sib_tiles, own_inverse, sib_inverse, *refs):
    count = SIDES * len(older) * CHAINS
    known, refs = refs[:count], refs[count:]
    base, refs = refs[: CHAINS * has_base], refs[CHAINS * has_base :]
    w_high, w_low, d_high, d_low, partial, buffer, sems = refs[n_after:]
    tiles, block = own_tiles.shape[0], own_tiles.shape[1]
    own = meta_ref[OWN_COLOUR] == now
    active = own | (meta_ref[SIB_COLOUR] == now)
    slots = [(newest, side) for side in range(SIDES)] + [(c, side) for c in older for side in range(SIDES)]

    @pl.when(active)
    def _():
        def fetch(own_src, sib_src, slot, start):
            @pl.when(own)
            def _():
                copy = pltpu.make_async_copy(own_src, buffer.at[slot], sems.at[slot])
                copy.start() if start else copy.wait()

            @pl.when(jnp.logical_not(own))
            def _():
                copy = pltpu.make_async_copy(sib_src, buffer.at[slot], sems.at[slot])
                copy.start() if start else copy.wait()

        which = [tile_of(meta_ref, own, tiles, c, side) for c, side in slots]
        fetch(own_inverse, sib_inverse, len(slots), True)
        for slot, k in enumerate(which):
            @pl.when(k >= 0)
            def _():
                fetch(own_tiles.at[k], sib_tiles.at[k], slot, True)

        if has_base:
            partial[...] = jnp.concatenate([b[...] for b in base], axis=0)
        else:
            partial[...] = jnp.zeros_like(partial)
        fetch(own_inverse, sib_inverse, len(slots), False)
        d_high[...], d_low[...] = split(buffer[len(slots)])
        for slot, k in enumerate(which):
            span = pl.ds(slot * block, block)

            @pl.when(k >= 0)
            def _():
                fetch(own_tiles.at[k], sib_tiles.at[k], slot, False)
                high, low = split(buffer[slot])
                if slot < SIDES:
                    w_high[:, span] = high
                    w_low[:, span] = low
                else:
                    at = (slot - SIDES) * CHAINS
                    value = jnp.concatenate([r[...] for r in known[at : at + CHAINS]], axis=0)
                    partial[...] += times(value, high, low)

            if slot < SIDES:
                @pl.when(k < 0)
                def _():
                    w_high[:, span] = jnp.zeros((block, block), jnp.bfloat16)
                    w_low[:, span] = jnp.zeros((block, block), jnp.bfloat16)


def relax_kernel(now, chain, meta_ref, w_high, w_low, d_high, d_low, partial, behind, here, ahead, own_start, sib_start, *refs):
    out_ref, sum_ref = refs[-2:]
    own = meta_ref[OWN_COLOUR] == now
    active = own | (meta_ref[SIB_COLOUR] == now)
    width = out_ref.shape[0]
    rows = pl.ds(chain * width, width)

    @pl.when(active)
    def _():
        value = jnp.concatenate([behind[...], here[...], ahead[...]], axis=1)
        coupled = partial[rows, :] + times(value, w_high[...], w_low[...])
        sum_ref[...] = coupled
        start = jnp.where(own, own_start[rows, :], sib_start[rows, :])
        out_ref[...] = start - times(coupled, d_high[...], d_low[...])


def gather(now, newest, older, meta, matrices, known, base, after):
    tiles, block, _ = matrices[0].shape
    width = known[newest][0][0].shape[0]
    slots = SIDES * (1 + len(older)) + 1
    operands = [known[c][chain][side] for c in older for side in range(SIDES) for chain in range(CHAINS)]
    operands = near(operands + (base or []))
    bf16 = jnp.bfloat16
    return pl.pallas_call(
        functools.partial(gather_kernel, now, newest, older, int(base is not None), len(after)),
        out_shape=[
            pltpu.VMEM((block, SIDES * block), bf16),
            pltpu.VMEM((block, SIDES * block), bf16),
            pltpu.VMEM((block, block), bf16),
            pltpu.VMEM((block, block), bf16),
            pltpu.VMEM((CHAINS * width, block), jnp.float32),
        ],
        in_specs=[smem()] + [anywhere()] * 4 + [vmem()] * len(operands) + [anywhere()] * len(after),
        out_specs=[vmem()] * 5,
        scratch_shapes=[
            pltpu.VMEM((slots, block, block), jnp.float32),
            pltpu.SemaphoreType.DMA((slots,)),
        ],
        compiler_params=params(),
        cost_estimate=pl.CostEstimate(
            flops=4 * block * block * 128 * slots, bytes_accessed=4 * block * block * slots, transcendentals=0
        ),
        name=f"gather_{now}_{newest}",
    )(meta, *matrices, *operands, *after)


def relax(now, chain, meta, gathered, latest, own_start, sib_start, after):
    block = gathered[2].shape[0]
    width = own_start.shape[0] // CHAINS
    operands = near([*gathered, *latest, own_start, sib_start])
    return pl.pallas_call(
        functools.partial(relax_kernel, now, chain),
        out_shape=[pltpu.VMEM((width, block), jnp.float32)] * 2,
        in_specs=[smem()] + [vmem()] * len(operands) + [anywhere()] * len(after),
        out_specs=[vmem()] * 2,
        compiler_params=params(),
        cost_estimate=pl.CostEstimate(
            flops=16 * block * block * 128, bytes_accessed=16 * block * block, transcendentals=0
        ),
        name=f"relax_{now}_{chain}",
    )(meta, *operands, *after)


def per_device(residual, inv_diag, coupling_tiles, colour, tile_cols):
    axis = "rows"
    count = lax.axis_size(axis)
    groups = count // COLOURS
    me = lax.axis_index(axis)
    core = (me % 2).reshape(1)
    place = me % COLOURS
    group = me // COLOURS
    block, cols = residual.shape
    half = cols // 2
    width = half // CHAINS
    tiles = jnp.transpose(coupling_tiles, (1, 0, 2))

    def flip(value, bit):
        return lax.ppermute(value, axis, [(i, i ^ bit) for i in range(count)])

    def shift(value, by):
        return lax.ppermute(value, axis, [(i, (i + by) % count) for i in range(count)])

    own_facts = jnp.concatenate([colour, tile_cols[0]])
    sib_facts = flip(own_facts, 1)
    own_colour, sib_colour = own_facts[0], sib_facts[0]

    late_residual, _ = lax.optimization_barrier((residual, own_facts))
    keep, send = pl.pallas_call(
        first_kernel,
        out_shape=[pltpu.VMEM((half, block), jnp.float32)] * 2,
        in_specs=[smem(), vmem(), vmem()],
        out_specs=[vmem()] * 2,
        compiler_params=params(),
        name="first",
    )(core, inv_diag, late_residual)
    own_start, sib_start = keep, flip(send, 1)

    candidate = jnp.where(own_colour == 0, own_start, sib_start)
    candidates = [candidate[c * width : (c + 1) * width] for c in range(CHAINS)]

    late_tiles, late_inverse, _, _ = lax.optimization_barrier((tiles, inv_diag, sib_start, sib_facts))
    matrices = [tiles, flip(late_tiles, 1), inv_diag, flip(late_inverse, 1)]

    def across(candidate, now):
        here_now = (own_colour == now) | (sib_colour == now)
        return jnp.where(here_now, candidate, flip(candidate, 2))

    def around(here):
        return [shift(here, COLOURS), here, shift(here, -COLOURS)]

    here = [across(c, 0) for c in candidates]

    wheel = jnp.arange(COLOURS, dtype=jnp.int32)
    pair_places = jnp.where(wheel == own_colour, place, 0) + jnp.where(wheel == sib_colour, place ^ 1, 0)
    pair_places, _ = lax.optimization_barrier((pair_places, candidates[0]))
    group_places = pair_places + flip(pair_places, 2)
    group_places, _ = lax.optimization_barrier((group_places, here[0]))
    places = [shift(group_places, COLOURS), group_places, shift(group_places, -COLOURS)]
    blocks = [(((group + side - 1) % groups) * COLOURS + places[side]).astype(jnp.int32) for side in range(SIDES)]
    meta = jnp.concatenate([own_facts[:1], sib_facts[:1], own_facts[1:], sib_facts[1:]] + blocks)

    known = {0: [around(h) for h in here]}
    order = list(range(1, COLOURS)) + list(range(COLOURS - 2, -1, -1))
    newest, done = 0, {0}
    sums, used, finals = {}, {}, {}
    previous = candidates
    for step, now in enumerate(order):
        fresh = used.get(now, set())
        older = tuple(c for c in sorted(known) if c not in (now, newest) and (c, done_at(order, c, step)) not in fresh)
        gathered = gather(now, newest, older, meta, matrices, known, sums.get(now), [previous[-1]] if step else [])
        used[now] = {(c, done_at(order, c, step)) for c in known if c != now}
        candidates, sums[now], here = [], [], []
        for chain in range(CHAINS):
            after = [here[-1] if here else candidates[-1]] if chain else []
            candidate, total = relax(now, chain, meta, gathered, known[newest][chain], own_start, sib_start, after)
            candidates.append(candidate)
            sums[now].append(total)
            if step < len(order) - 1:
                here.append(across(candidate, now))
        finals[now] = candidates
        if here:
            known[now] = [around(h) for h in here]
        newest, previous = now, candidates

    own_final, sib_final = finals[0], finals[0]
    for c in range(1, COLOURS):
        own_final = [jnp.where(own_colour == c, a, b) for a, b in zip(finals[c], own_final)]
        sib_final = [jnp.where(sib_colour == c, a, b) for a, b in zip(finals[c], sib_final)]
    mine, other = jnp.concatenate(own_final), flip(jnp.concatenate(sib_final), 1)
    return pl.pallas_call(
        last_kernel,
        out_shape=jax.ShapeDtypeStruct((block, cols), jnp.float32),
        in_specs=[smem(), vmem(), vmem()],
        out_specs=vmem(),
        compiler_params=params(),
        name="last",
    )(core, *near([mine, other]))


def done_at(order, colour, step):
    return max([i for i in range(step) if order[i] == colour], default=-1)


def solution(mesh):
    in_specs = (P("rows", None), P("rows", None), P("rows", None, None), P("rows"), P("rows", None))
    out_specs = P("rows", None)
    return jax.shard_map(
        per_device, mesh=mesh, in_specs=in_specs, out_specs=out_specs, check_vma=False
    )
```

```python
import functools

import jax
import jax.numpy as jnp
from jax import lax
from jax.experimental import pallas as pl
from jax.experimental.pallas import tpu as pltpu
from jax.sharding import PartitionSpec as P

COLOURS = 4
SIDES = 3
PIECES = 2
EXTRA = 8
OWN_COLOUR = 0
SIB_COLOUR = 1
TILE_START = 2


def dot_t(a, b):
    return lax.dot_general(a, b, (((1,), (1,)), ((), ())), preferred_element_type=jnp.float32)


def split(value):
    high = value.astype(jnp.bfloat16)
    return high, (value - high.astype(jnp.float32)).astype(jnp.bfloat16)


def times(value, high, low):
    rows = value.shape[0]
    parts = jnp.concatenate(split(value), axis=0)
    product = dot_t(parts, high) + dot_t(parts, low)
    return product[:rows] + product[rows:]


def vmem():
    return pl.BlockSpec(memory_space=pltpu.VMEM)


def smem():
    return pl.BlockSpec(memory_space=pltpu.SMEM)


def anywhere():
    return pl.BlockSpec(memory_space=pl.ANY)


def hbm():
    return pl.BlockSpec(memory_space=pltpu.HBM)


def params(mebibytes):
    return pltpu.CompilerParams(vmem_limit_bytes=mebibytes * 1024 * 1024)


def far(values):
    return [pltpu.with_memory_space_constraint(v, pltpu.HBM) for v in values]


def near(values):
    return [pltpu.with_memory_space_constraint(v, pltpu.VMEM) for v in values]


def whole(pieces, half):
    return jnp.concatenate([piece[: half // len(pieces), :] for piece in pieces], axis=0)


def first_kernel(facts_ref, inverse_hbm, residual_hbm, keep_ref, send_ref, inverse_ref, residual_ref, sems):
    copies = [
        pltpu.make_async_copy(residual_hbm, residual_ref, sems.at[0]),
        pltpu.make_async_copy(inverse_hbm, inverse_ref, sems.at[1]),
    ]
    for copy in copies:
        copy.start()
    for copy in copies:
        copy.wait()
    value = times(jnp.transpose(residual_ref[...]), *split(inverse_ref[...]))
    half, block = keep_ref.shape
    is_first = facts_ref[0] == 0
    keep_ref[...] = jnp.where(is_first, value[:half], value[half:])
    send_ref[:half, :] = jnp.where(is_first, value[half:], value[:half])
    row = lax.broadcasted_iota(jnp.int32, (EXTRA, block), 0)
    rows = jnp.zeros((EXTRA, block), jnp.int32)
    for i in range(1, facts_ref.shape[0]):
        rows = jnp.where(row == i - 1, facts_ref[i], rows)
    send_ref[half:, :] = rows.astype(jnp.float32)


def last_kernel(core_ref, mine_ref, other_ref, out_ref):
    is_first = core_ref[0] == 0
    mine, other = mine_ref[...], other_ref[...]
    first = jnp.where(is_first, mine, other)
    second = jnp.where(is_first, other, mine)
    out_ref[...] = jnp.transpose(jnp.concatenate([first, second], axis=0))


def tile_of(meta_ref, own, tiles, colour, side):
    wanted = meta_ref[TILE_START + 2 * tiles + side * COLOURS + colour]
    start = jnp.where(own, TILE_START, TILE_START + tiles)
    found = jnp.int32(-1)
    for k in range(tiles):
        found = jnp.where(meta_ref[start + k] == wanted, k, found)
    return found


def gather_kernel(now, newest, older, counts, has_base, n_after, meta_ref, own_tiles, sib_tiles, own_inverse, sib_inverse, own_start, sib_start, *refs):
    known = []
    for count in counts:
        known += [refs[side * count : (side + 1) * count] for side in range(SIDES)]
        refs = refs[SIDES * count :]
    base, refs = refs[:has_base], refs[has_base:]
    w_high, w_low, d_high, d_low, partial, begin, flag, buffer, sems = refs[n_after:]
    tiles, block = own_tiles.shape[0], own_tiles.shape[1]
    half = begin.shape[0]
    own = meta_ref[OWN_COLOUR] == now
    active = own | (meta_ref[SIB_COLOUR] == now)
    slots = [(newest, side) for side in range(SIDES)] + [(c, side) for c in older for side in range(SIDES)]
    flag[...] = jnp.broadcast_to(active.astype(jnp.int32), flag.shape)

    @pl.when(active)
    def _():
        def fetch(own_src, sib_src, slot, start):
            @pl.when(own)
            def _():
                copy = pltpu.make_async_copy(own_src, buffer.at[slot], sems.at[slot])
                copy.start() if start else copy.wait()

            @pl.when(jnp.logical_not(own))
            def _():
                copy = pltpu.make_async_copy(sib_src, buffer.at[slot], sems.at[slot])
                copy.start() if start else copy.wait()

        which = [tile_of(meta_ref, own, tiles, c, side) for c, side in slots]
        fetch(own_inverse, sib_inverse, len(slots), True)
        for slot, k in enumerate(which):
            @pl.when(k >= 0)
            def _():
                fetch(own_tiles.at[k], sib_tiles.at[k], slot, True)

        begin[...] = jnp.where(own, own_start[...], sib_start[:half, :])
        partial[...] = base[0][...] if has_base else jnp.zeros_like(partial)
        fetch(own_inverse, sib_inverse, len(slots), False)
        d_high[...], d_low[...] = split(buffer[len(slots)])
        for slot, k in enumerate(which):
            span = pl.ds(slot * block, block)

            @pl.when(k >= 0)
            def _():
                fetch(own_tiles.at[k], sib_tiles.at[k], slot, False)
                high, low = split(buffer[slot])
                if slot < SIDES:
                    w_high[:, span] = high
                    w_low[:, span] = low
                else:
                    partial[...] += times(whole(known[slot - SIDES], half), high, low)

            if slot < SIDES:
                @pl.when(k < 0)
                def _():
                    w_high[:, span] = jnp.zeros((block, block), jnp.bfloat16)
                    w_low[:, span] = jnp.zeros((block, block), jnp.bfloat16)


def relax_kernel(count, flag, w_high, w_low, d_high, d_low, partial, begin, *refs):
    latest, outs = refs[: SIDES * count], refs[SIDES * count :]
    half = begin.shape[0]
    width = outs[0].shape[0]

    @pl.when(flag[0, 0] != 0)
    def _():
        sides = [whole(latest[side * count : (side + 1) * count], half) for side in range(SIDES)]
        value = jnp.concatenate(sides, axis=1)
        coupled = partial[...] + times(value, w_high[...], w_low[...])
        for ref in outs[PIECES:]:
            ref[...] = coupled
        result = begin[...] - times(coupled, d_high[...], d_low[...])
        for piece in range(PIECES):
            outs[piece][...] = result[piece * width : (piece + 1) * width]


def gather(now, newest, older, meta, matrices, starts, known, base, after):
    tiles, block, _ = matrices[0].shape
    half = starts[0].shape[0]
    slots = SIDES * (1 + len(older)) + 1
    operands = [piece[side] for c in older for side in range(SIDES) for piece in known[c]]
    operands = near([*starts, *operands, *base])
    counts = [len(known[c]) for c in older]
    bf16 = jnp.bfloat16
    return pl.pallas_call(
        functools.partial(gather_kernel, now, newest, older, counts, len(base), len(after)),
        out_shape=[
            pltpu.VMEM((block, SIDES * block), bf16),
            pltpu.VMEM((block, SIDES * block), bf16),
            pltpu.VMEM((block, block), bf16),
            pltpu.VMEM((block, block), bf16),
            pltpu.VMEM((half, block), jnp.float32),
            pltpu.VMEM((half, block), jnp.float32),
            pltpu.VMEM((8, 128), jnp.int32),
        ],
        in_specs=[smem()] + [hbm(), anywhere()] * 2 + [vmem()] * len(operands) + [anywhere()] * len(after),
        out_specs=[vmem()] * 7,
        scratch_shapes=[
            pltpu.VMEM((slots, block, block), jnp.float32),
            pltpu.SemaphoreType.DMA((slots,)),
        ],
        compiler_params=params(28),
        cost_estimate=pl.CostEstimate(
            flops=4 * block * block * 128 * slots, bytes_accessed=4 * block * block * slots, transcendentals=0
        ),
        name=f"gather_{now}_{newest}",
    )(meta, *matrices, *operands, *after)


def relax(now, gathered, latest, keep_sum):
    *weights, partial, begin, flag = gathered
    half, block = begin.shape
    operands = [piece[side] for side in range(SIDES) for piece in latest]
    operands = near([flag, *weights, partial, begin, *operands])
    out_shape = [pltpu.VMEM((half // PIECES, block), jnp.float32)] * PIECES
    out_shape += [pltpu.VMEM((half, block), jnp.float32)] * keep_sum
    return pl.pallas_call(
        functools.partial(relax_kernel, len(latest)),
        out_shape=out_shape,
        in_specs=[vmem()] * len(operands),
        out_specs=[vmem()] * len(out_shape),
        compiler_params=params(16),
        cost_estimate=pl.CostEstimate(
            flops=16 * block * block * 128, bytes_accessed=16 * block * block, transcendentals=0
        ),
        name=f"relax_{now}",
    )(*operands)


def per_device(residual, inv_diag, coupling_tiles, colour, tile_cols):
    axis = "rows"
    count = lax.axis_size(axis)
    groups = count // COLOURS
    me = lax.axis_index(axis)
    core = (me % 2).reshape(1)
    place = me % COLOURS
    group = me // COLOURS
    block, cols = residual.shape
    half = cols // 2
    tiles = jnp.transpose(coupling_tiles, (1, 0, 2))
    number = tiles.shape[0]

    def flip(value, bit):
        return lax.ppermute(value, axis, [(i, i ^ bit) for i in range(count)])

    def shift(value, by):
        return lax.ppermute(value, axis, [(i, (i + by) % count) for i in range(count)])

    def across(candidates, here_now):
        swapped = [flip(c, 2) for c in candidates]
        return [jnp.where(here_now, c, s) for c, s in zip(candidates, swapped)], swapped

    def around(here):
        return [[shift(h, COLOURS), h, shift(h, -COLOURS)] for h in here]

    facts = jnp.concatenate([core, colour, tile_cols[0]])
    keep, send = pl.pallas_call(
        first_kernel,
        out_shape=[pltpu.VMEM((half, block), jnp.float32), pltpu.VMEM((half + EXTRA, block), jnp.float32)],
        in_specs=[smem(), hbm(), hbm()],
        out_specs=[vmem()] * 2,
        scratch_shapes=[
            pltpu.VMEM((block, block), jnp.float32),
            pltpu.VMEM((block, cols), jnp.float32),
            pltpu.SemaphoreType.DMA((2,)),
        ],
        compiler_params=params(16),
        name="first",
    )(facts, *far([inv_diag, residual]))
    arrived = flip(send, 1)
    starts = [keep, arrived]
    own_colour = colour[0]
    sib_facts = arrived[half : half + 1 + number, 0].astype(jnp.int32)
    sib_colour = sib_facts[0]

    late_tiles, late_inverse, _ = lax.optimization_barrier((tiles, inv_diag, arrived))
    own_tiles, own_inverse = far([tiles, inv_diag])
    matrices = [own_tiles, flip(late_tiles, 1), own_inverse, flip(late_inverse, 1)]

    candidate = jnp.where(own_colour == 0, keep, arrived[:half])
    wheel = lax.broadcasted_iota(jnp.int32, (EXTRA, block), 0)
    sib_wide = arrived[half : half + 1]
    places = jnp.where(wheel == own_colour, place, 0) + jnp.where(wheel.astype(jnp.float32) == sib_wide, place ^ 1, 0)
    places = places.astype(jnp.float32)
    here, swapped = across([jnp.concatenate([candidate, places])], (own_colour == 0) | (sib_colour == 0))
    known = {0: around([jnp.concatenate([here[0][:half], places + swapped[0][half:]])])}
    blocks = []
    for side in range(SIDES):
        found = known[0][0][side][half : half + COLOURS, 0].astype(jnp.int32)
        blocks.append((((group + side - 1) % groups) * COLOURS + found).astype(jnp.int32))
    meta = jnp.concatenate([colour, sib_facts[:1], tile_cols[0], sib_facts[1:]] + blocks)

    order = list(range(1, COLOURS)) + list(range(COLOURS - 2, -1, -1))
    newest = 0
    sums, used, finals = {}, {}, {}
    after = []
    for step, now in enumerate(order):
        fresh = used.get(now, set())
        older = tuple(c for c in sorted(known) if c not in (now, newest) and (c, done_at(order, c, step)) not in fresh)
        gathered = gather(now, newest, older, meta, matrices, starts, known, sums.get(now, []), after)
        used[now] = {(c, done_at(order, c, step)) for c in known if c != now}
        outs = relax(now, gathered, known[newest], int(now in order[step + 1 :]))
        candidates, sums[now] = outs[:PIECES], outs[PIECES:]
        finals[now], after, newest = candidates, candidates[:1], now
        if step < len(order) - 1:
            here, _ = across(candidates, (own_colour == now) | (sib_colour == now))
            known[now] = around(here)

    own_final, sib_final = finals[0], finals[0]
    for c in range(1, COLOURS):
        own_final = [jnp.where(own_colour == c, a, b) for a, b in zip(finals[c], own_final)]
        sib_final = [jnp.where(sib_colour == c, a, b) for a, b in zip(finals[c], sib_final)]
    mine, other = jnp.concatenate(own_final), flip(jnp.concatenate(sib_final), 1)
    return pl.pallas_call(
        last_kernel,
        out_shape=jax.ShapeDtypeStruct((block, cols), jnp.float32),
        in_specs=[smem(), vmem(), vmem()],
        out_specs=vmem(),
        compiler_params=params(16),
        name="last",
    )(core, *near([mine, other]))


def done_at(order, colour, step):
    return max([i for i in range(step) if order[i] == colour], default=-1)


def solution(mesh):
    in_specs = (P("rows", None), P("rows", None), P("rows", None, None), P("rows"), P("rows", None))
    out_specs = P("rows", None)
    return jax.shard_map(
        per_device, mesh=mesh, in_specs=in_specs, out_specs=out_specs, check_vma=False
    )
```

```python
import functools

import jax
import jax.numpy as jnp
from jax import lax
from jax.experimental import pallas as pl
from jax.experimental.pallas import tpu as pltpu
from jax.sharding import PartitionSpec as P

COLOURS = 4
SIDES = 3
CHIPS = 2
EXTRA = 8
OWN_COLOUR = 0
SIB_COLOUR = 1
PARITY = 2
TILE_START = 3


def dot_t(a, b):
    return lax.dot_general(a, b, (((1,), (1,)), ((), ())), preferred_element_type=jnp.float32)


def split(value):
    high = value.astype(jnp.bfloat16)
    return high, (value - high.astype(jnp.float32)).astype(jnp.bfloat16)


def times(value, high, low):
    rows = value.shape[0]
    parts = jnp.concatenate(split(value), axis=0)
    product = dot_t(parts, high) + dot_t(parts, low)
    return product[:rows] + product[rows:]


def vmem():
    return pl.BlockSpec(memory_space=pltpu.VMEM)


def smem():
    return pl.BlockSpec(memory_space=pltpu.SMEM)


def anywhere():
    return pl.BlockSpec(memory_space=pl.ANY)


def hbm():
    return pl.BlockSpec(memory_space=pltpu.HBM)


def params(mebibytes):
    return pltpu.CompilerParams(vmem_limit_bytes=mebibytes * 1024 * 1024)


def far(values):
    return [pltpu.with_memory_space_constraint(v, pltpu.HBM) for v in values]


def near(values):
    return [pltpu.with_memory_space_constraint(v, pltpu.VMEM) for v in values]


def pick(gathered, parity, chip, side, half):
    early, late = gathered
    stride = early.shape[0] // (2 * CHIPS)
    entry = chip + (2 * parity if side == 1 else CHIPS * (side // 2))
    rows = pl.ds(pl.multiple_of(entry * stride, 8), half)
    if side == 1:
        return early[rows, :]
    return jnp.where((parity == 0) == (side == 2), early[rows, :], late[rows, :])


def first_kernel(facts_ref, inverse_hbm, residual_hbm, keep_ref, send_ref, inverse_ref, residual_ref, sems):
    copies = [
        pltpu.make_async_copy(residual_hbm, residual_ref, sems.at[0]),
        pltpu.make_async_copy(inverse_hbm, inverse_ref, sems.at[1]),
    ]
    for copy in copies:
        copy.start()
    for copy in copies:
        copy.wait()
    value = times(jnp.transpose(residual_ref[...]), *split(inverse_ref[...]))
    half, block = keep_ref.shape
    is_first = facts_ref[0] == 0
    keep_ref[...] = jnp.where(is_first, value[:half], value[half:])
    send_ref[:half, :] = jnp.where(is_first, value[half:], value[:half])
    row = lax.broadcasted_iota(jnp.int32, (EXTRA, block), 0)
    rows = jnp.zeros((EXTRA, block), jnp.int32)
    for i in range(1, facts_ref.shape[0]):
        rows = jnp.where(row == i - 1, facts_ref[i], rows)
    send_ref[half:, :] = rows.astype(jnp.float32)


def last_kernel(core_ref, mine_ref, other_ref, out_ref):
    is_first = core_ref[0] == 0
    mine, other = mine_ref[...], other_ref[...]
    first = jnp.where(is_first, mine, other)
    second = jnp.where(is_first, other, mine)
    out_ref[...] = jnp.transpose(jnp.concatenate([first, second], axis=0))


def ids(tiles, side, colour):
    return TILE_START + 2 * tiles + side * COLOURS + colour


def tile_of(meta_ref, own, tiles, colour, side):
    wanted = meta_ref[ids(tiles, side, colour)]
    start = jnp.where(own, TILE_START, TILE_START + tiles)
    found = jnp.int32(-1)
    for k in range(tiles):
        found = jnp.where(meta_ref[start + k] == wanted, k, found)
    return found


def gather_kernel(now, newest, older, has_base, n_after, meta_ref, own_tiles, sib_tiles, own_inverse, sib_inverse, own_start, sib_start, *refs):
    known, refs = refs[: 2 * len(older)], refs[2 * len(older) :]
    base, refs = refs[:has_base], refs[has_base:]
    w_high, w_low, d_high, d_low, partial, begin, flag, buffer, sems = refs[n_after:]
    tiles, block = own_tiles.shape[0], own_tiles.shape[1]
    half = begin.shape[0]
    own = meta_ref[OWN_COLOUR] == now
    active = own | (meta_ref[SIB_COLOUR] == now)
    slots = [(newest, side) for side in range(SIDES)] + [(c, side) for c in older for side in range(SIDES)]
    parity = meta_ref[PARITY]
    chips = [[(meta_ref[ids(tiles, side, c)] >> 1) & 1 for side in range(SIDES)] for c in range(COLOURS)]
    row = lax.broadcasted_iota(jnp.int32, flag.shape, 0)
    marks = jnp.zeros(flag.shape, jnp.int32)
    for i, mark in enumerate([active.astype(jnp.int32), parity, *chips[newest]]):
        marks = jnp.where(row == i, mark, marks)
    flag[...] = marks

    @pl.when(active)
    def _():
        def fetch(own_src, sib_src, slot, start):
            @pl.when(own)
            def _():
                copy = pltpu.make_async_copy(own_src, buffer.at[slot], sems.at[slot])
                copy.start() if start else copy.wait()

            @pl.when(jnp.logical_not(own))
            def _():
                copy = pltpu.make_async_copy(sib_src, buffer.at[slot], sems.at[slot])
                copy.start() if start else copy.wait()

        which = [tile_of(meta_ref, own, tiles, c, side) for c, side in slots]
        fetch(own_inverse, sib_inverse, len(slots), True)
        for slot, k in enumerate(which):
            @pl.when(k >= 0)
            def _():
                fetch(own_tiles.at[k], sib_tiles.at[k], slot, True)

        begin[...] = jnp.where(own, own_start[...], sib_start[:half, :])
        partial[...] = base[0][...] if has_base else jnp.zeros_like(partial)
        fetch(own_inverse, sib_inverse, len(slots), False)
        d_high[...], d_low[...] = split(buffer[len(slots)])
        for slot, k in enumerate(which):
            span = pl.ds(slot * block, block)

            @pl.when(k >= 0)
            def _():
                fetch(own_tiles.at[k], sib_tiles.at[k], slot, False)
                high, low = split(buffer[slot])
                if slot < SIDES:
                    w_high[:, span] = high
                    w_low[:, span] = low
                else:
                    at = (slot - SIDES) // SIDES * 2
                    c, side = slots[slot]
                    partial[...] += times(pick(known[at : at + 2], parity, chips[c][side], side, half), high, low)

            if slot < SIDES:
                @pl.when(k < 0)
                def _():
                    w_high[:, span] = jnp.zeros((block, block), jnp.bfloat16)
                    w_low[:, span] = jnp.zeros((block, block), jnp.bfloat16)


def relax_kernel(flag, w_high, w_low, d_high, d_low, partial, begin, early, late, out, *total):
    half = begin.shape[0]

    @pl.when(flag[0, 0] != 0)
    def _():
        sides = [pick((early, late), flag[1, 0], flag[2 + side, 0], side, half) for side in range(SIDES)]
        coupled = partial[...] + times(jnp.concatenate(sides, axis=1), w_high[...], w_low[...])
        for ref in total:
            ref[...] = coupled
        out[...] = begin[...] - times(coupled, d_high[...], d_low[...])


def gather(now, newest, older, meta, matrices, starts, known, base, after):
    tiles, block, _ = matrices[0].shape
    half = starts[0].shape[0]
    slots = SIDES * (1 + len(older)) + 1
    operands = [value for c in older for value in known[c]]
    operands = near([*starts, *operands, *base])
    bf16 = jnp.bfloat16
    return pl.pallas_call(
        functools.partial(gather_kernel, now, newest, older, len(base), len(after)),
        out_shape=[
            pltpu.VMEM((block, SIDES * block), bf16),
            pltpu.VMEM((block, SIDES * block), bf16),
            pltpu.VMEM((block, block), bf16),
            pltpu.VMEM((block, block), bf16),
            pltpu.VMEM((half, block), jnp.float32),
            pltpu.VMEM((half, block), jnp.float32),
            pltpu.VMEM((8, 128), jnp.int32),
        ],
        in_specs=[smem()] + [hbm(), anywhere()] * 2 + [vmem()] * len(operands) + [anywhere()] * len(after),
        out_specs=[vmem()] * 7,
        scratch_shapes=[
            pltpu.VMEM((slots, block, block), jnp.float32),
            pltpu.SemaphoreType.DMA((slots,)),
        ],
        compiler_params=params(28),
        cost_estimate=pl.CostEstimate(
            flops=4 * block * block * 128 * slots, bytes_accessed=4 * block * block * slots, transcendentals=0
        ),
        name=f"gather_{now}_{newest}",
    )(meta, *matrices, *operands, *after)


def relax(now, gathered, latest, keep_sum):
    *weights, partial, begin, flag = gathered
    half, block = begin.shape
    operands = near([flag, *weights, partial, begin, *latest])
    out_shape = [pltpu.VMEM((half, block), jnp.float32)] * (1 + keep_sum)
    return pl.pallas_call(
        relax_kernel,
        out_shape=out_shape,
        in_specs=[vmem()] * len(operands),
        out_specs=[vmem()] * len(out_shape),
        compiler_params=params(16),
        cost_estimate=pl.CostEstimate(
            flops=16 * block * block * 128, bytes_accessed=16 * block * block, transcendentals=0
        ),
        name=f"relax_{now}",
    )(*operands)


def per_device(residual, inv_diag, coupling_tiles, colour, tile_cols):
    axis = "rows"
    count = lax.axis_size(axis)
    groups = count // COLOURS
    me = lax.axis_index(axis)
    core = (me % 2).reshape(1)
    place = me % COLOURS
    group = me // COLOURS
    block, cols = residual.shape
    half = cols // 2
    tiles = jnp.transpose(coupling_tiles, (1, 0, 2))
    number = tiles.shape[0]

    def flip(value, bit):
        return lax.ppermute(value, axis, [(i, i ^ bit) for i in range(count)])

    def spread(value):
        gathers = []
        for offset in range(2):
            sets = []
            for start in range(offset, groups + offset, 2):
                for one in range(COLOURS // CHIPS):
                    sets.append([(start * COLOURS + one + (COLOURS // CHIPS) * i) % count for i in range(2 * CHIPS)])
            gathers.append(lax.all_gather(value, axis, axis_index_groups=sets, tiled=True))
        return gathers

    facts = jnp.concatenate([core, colour, tile_cols[0]])
    keep, send = pl.pallas_call(
        first_kernel,
        out_shape=[pltpu.VMEM((half, block), jnp.float32), pltpu.VMEM((half + EXTRA, block), jnp.float32)],
        in_specs=[smem(), hbm(), hbm()],
        out_specs=[vmem()] * 2,
        scratch_shapes=[
            pltpu.VMEM((block, block), jnp.float32),
            pltpu.VMEM((block, cols), jnp.float32),
            pltpu.SemaphoreType.DMA((2,)),
        ],
        compiler_params=params(16),
        name="first",
    )(facts, *far([inv_diag, residual]))
    arrived = flip(send, 1)
    starts = [keep, arrived]
    own_colour = colour[0]
    sib_facts = arrived[half : half + 1 + number, 0].astype(jnp.int32)
    sib_colour = sib_facts[0]

    late_tiles, late_inverse, _ = lax.optimization_barrier((tiles, inv_diag, arrived))
    own_tiles, own_inverse = far([tiles, inv_diag])
    matrices = [own_tiles, flip(late_tiles, 1), own_inverse, flip(late_inverse, 1)]

    candidate = jnp.where(own_colour == 0, keep, arrived[:half])
    wheel = lax.broadcasted_iota(jnp.int32, (EXTRA, block), 0)
    sib_wide = arrived[half : half + 1]
    places = jnp.where(wheel == own_colour, place, 0) + jnp.where(wheel.astype(jnp.float32) == sib_wide, place ^ 1, 0)
    places = places.astype(jnp.float32)
    known = {0: spread(jnp.concatenate([candidate, places]))}
    parity = group % 2
    blocks = []
    tables = [g.reshape(2, CHIPS, half + EXTRA, block)[:, :, half : half + COLOURS, 0].sum(1).astype(jnp.int32) for g in known[0]]
    found = [
        jnp.where(parity == 0, tables[1][0], tables[0][0]),
        jnp.where(parity == 0, tables[0][0], tables[0][1]),
        jnp.where(parity == 0, tables[0][1], tables[1][1]),
    ]
    for side in range(SIDES):
        blocks.append((((group + side - 1) % groups) * COLOURS + found[side]).astype(jnp.int32))
    meta = jnp.concatenate([colour, sib_facts[:1], parity.reshape(1), tile_cols[0], sib_facts[1:]] + blocks)

    order = list(range(1, COLOURS)) + list(range(COLOURS - 2, -1, -1))
    newest = 0
    sums, used, finals = {}, {}, {}
    after = []
    for step, now in enumerate(order):
        fresh = used.get(now, set())
        older = tuple(c for c in sorted(known) if c not in (now, newest) and (c, done_at(order, c, step)) not in fresh)
        gathered = gather(now, newest, older, meta, matrices, starts, known, sums.get(now, []), after)
        used[now] = {(c, done_at(order, c, step)) for c in known if c != now}
        outs = relax(now, gathered, known[newest], int(now in order[step + 1 :]))
        finals[now], sums[now] = outs[0], outs[1:]
        after, newest = [outs[0]], now
        if step < len(order) - 1:
            known[now] = spread(outs[0])

    own_final, sib_final = finals[0], finals[0]
    for c in range(1, COLOURS):
        own_final = jnp.where(own_colour == c, finals[c], own_final)
        sib_final = jnp.where(sib_colour == c, finals[c], sib_final)
    mine, other = own_final, flip(sib_final, 1)
    return pl.pallas_call(
        last_kernel,
        out_shape=jax.ShapeDtypeStruct((block, cols), jnp.float32),
        in_specs=[smem(), vmem(), vmem()],
        out_specs=vmem(),
        compiler_params=params(16),
        name="last",
    )(core, *near([mine, other]))


def done_at(order, colour, step):
    return max([i for i in range(step) if order[i] == colour], default=-1)


def solution(mesh):
    in_specs = (P("rows", None), P("rows", None), P("rows", None, None), P("rows"), P("rows", None))
    out_specs = P("rows", None)
    return jax.shard_map(
        per_device, mesh=mesh, in_specs=in_specs, out_specs=out_specs, check_vma=False
    )
```

```python
import functools

import jax
import jax.numpy as jnp
from jax import lax
from jax.experimental import pallas as pl
from jax.experimental.pallas import tpu as pltpu
from jax.sharding import PartitionSpec as P

COLOURS = 4
SIDES = 3
ORDER = (0, 2, 1)
PIECES = 2
EXTRA = 8
OWN_COLOUR = 0
SIB_COLOUR = 1
TILE_START = 2


def dot_t(a, b):
    return lax.dot_general(a, b, (((1,), (1,)), ((), ())), preferred_element_type=jnp.float32)


def split(value):
    high = value.astype(jnp.bfloat16)
    return high, (value - high.astype(jnp.float32)).astype(jnp.bfloat16)


def times(value, high, low):
    rows = value.shape[0]
    parts = jnp.concatenate(split(value), axis=0)
    product = dot_t(parts, high) + dot_t(parts, low)
    return product[:rows] + product[rows:]


def vmem():
    return pl.BlockSpec(memory_space=pltpu.VMEM)


def smem():
    return pl.BlockSpec(memory_space=pltpu.SMEM)


def anywhere():
    return pl.BlockSpec(memory_space=pl.ANY)


def hbm():
    return pl.BlockSpec(memory_space=pltpu.HBM)


def params(mebibytes):
    return pltpu.CompilerParams(vmem_limit_bytes=mebibytes * 1024 * 1024)


def far(values):
    return [pltpu.with_memory_space_constraint(v, pltpu.HBM) for v in values]


def near(values):
    return [pltpu.with_memory_space_constraint(v, pltpu.VMEM) for v in values]


def whole(pieces, half):
    return jnp.concatenate([piece[: half // len(pieces), :] for piece in pieces], axis=0)


def first_kernel(facts_ref, inverse_hbm, residual_hbm, keep_ref, send_ref, facts_out, inverse_ref, residual_ref, sems):
    copies = [
        pltpu.make_async_copy(residual_hbm, residual_ref, sems.at[0]),
        pltpu.make_async_copy(inverse_hbm, inverse_ref, sems.at[1]),
    ]
    for copy in copies:
        copy.start()
    for copy in copies:
        copy.wait()
    value = times(jnp.transpose(residual_ref[...]), *split(inverse_ref[...]))
    half, block = keep_ref.shape
    is_first = facts_ref[0] == 0
    keep_ref[...] = jnp.where(is_first, value[:half], value[half:])
    send_ref[:half, :] = jnp.where(is_first, value[half:], value[:half])
    row = lax.broadcasted_iota(jnp.int32, (EXTRA, block), 0)
    rows = jnp.zeros((EXTRA, block), jnp.int32)
    for i in range(1, facts_ref.shape[0]):
        rows = jnp.where(row == i - 1, facts_ref[i], rows)
    send_ref[half:, :] = rows.astype(jnp.float32)
    facts_out[...] = rows.astype(jnp.float32)


def last_kernel(core_ref, mine_ref, other_ref, out_ref):
    is_first = core_ref[0] == 0
    mine, other = mine_ref[...], other_ref[...]
    first = jnp.where(is_first, mine, other)
    second = jnp.where(is_first, other, mine)
    out_ref[...] = jnp.transpose(jnp.concatenate([first, second], axis=0))


def tile_of(meta_ref, own, tiles, colour, side):
    wanted = meta_ref[TILE_START + 2 * tiles + side * COLOURS + colour]
    start = jnp.where(own, TILE_START, TILE_START + tiles)
    found = jnp.int32(-1)
    for k in range(tiles):
        found = jnp.where(meta_ref[start + k] == wanted, k, found)
    return found


def mover(own, own_src, sib_src, dst, sem):
    def move(act):
        for is_own, src in ((own, own_src), (jnp.logical_not(own), sib_src)):
            @pl.when(is_own)
            def _(src=src):
                act(pltpu.make_async_copy(src, dst, sem))

    return move


def start(copy):
    copy.start()


def wait(copy):
    copy.wait()


def is_active(meta_ref, now):
    return (meta_ref[OWN_COLOUR] == now) | (meta_ref[SIB_COLOUR] == now)


def fetch_kernel(now, before, newest, n_after, meta_ref, own_tiles, sib_tiles, own_inverse, sib_inverse, own_start, sib_start, *refs):
    w_high, w_low, d_high, d_low, begin, mask, mask_before, buffer, sems = refs[n_after:]
    tiles, block = own_tiles.shape[0], own_tiles.shape[1]
    half = begin.shape[0]
    own = meta_ref[OWN_COLOUR] == now
    active = is_active(meta_ref, now)
    mask[...] = jnp.broadcast_to(active.astype(jnp.int32), mask.shape)
    mask_before[...] = jnp.broadcast_to(is_active(meta_ref, before).astype(jnp.int32), mask.shape)

    @pl.when(active)
    def _():
        which = [tile_of(meta_ref, own, tiles, newest, side) for side in ORDER]
        moves = [mover(own, own_tiles.at[k], sib_tiles.at[k], buffer.at[i], sems.at[i]) for i, k in enumerate(which)]
        moves.append(mover(own, own_inverse, sib_inverse, buffer.at[SIDES], sems.at[SIDES]))
        moves[-1](start)
        for k, move in zip(which, moves):
            @pl.when(k >= 0)
            def _():
                move(start)

        begin[...] = jnp.where(own, own_start[...], sib_start[:half, :])
        moves[-1](wait)
        d_high[...], d_low[...] = split(buffer[SIDES])
        for i, k in enumerate(which):
            span = pl.ds(i * block, block)

            @pl.when(k >= 0)
            def _():
                moves[i](wait)
                w_high[:, span], w_low[:, span] = split(buffer[i])

            @pl.when(k < 0)
            def _():
                w_high[:, span] = jnp.zeros((block, block), jnp.bfloat16)
                w_low[:, span] = jnp.zeros((block, block), jnp.bfloat16)


def older_kernel(now, older, counts, has_base, meta_ref, own_tiles, sib_tiles, w_high, w_low, *refs):
    *refs, partial, buffer, sems = refs
    here, refs = refs[: counts[0]], refs[counts[0] :]
    known = []
    for count in counts[1:]:
        known += [refs[side * count : (side + 1) * count] for side in range(SIDES)]
        refs = refs[SIDES * count :]
    tiles, block = own_tiles.shape[0], own_tiles.shape[1]
    half = partial.shape[0]
    own = meta_ref[OWN_COLOUR] == now

    @pl.when(is_active(meta_ref, now))
    def _():
        which = [tile_of(meta_ref, own, tiles, c, side) for c in older for side in range(SIDES)]
        moves = [mover(own, own_tiles.at[k], sib_tiles.at[k], buffer.at[i], sems.at[i]) for i, k in enumerate(which)]
        for k, move in zip(which, moves):
            @pl.when(k >= 0)
            def _():
                move(start)

        span = pl.ds((SIDES - 1) * block, block)
        total = times(whole(here, half), w_high[:, span], w_low[:, span])
        partial[...] = refs[0][...] + total if has_base else total
        for i, k in enumerate(which):
            @pl.when(k >= 0)
            def _():
                moves[i](wait)
                partial[...] += times(whole(known[i], half), *split(buffer[i]))


def relax_kernel(count, sides, mask, w_high, w_low, d_high, d_low, begin, *refs):
    latest, refs = refs[: sides * count], refs[sides * count :]
    if sides < SIDES:
        partial, *outs = refs
    else:
        partial, outs = None, refs
    half, block = begin.shape
    width = outs[0].shape[0]

    @pl.when(mask[0, 0] != 0)
    def _():
        values = [whole(latest[side * count : (side + 1) * count], half) for side in range(sides)]
        span = pl.ds(0, sides * block)
        coupled = times(jnp.concatenate(values, axis=1), w_high[:, span], w_low[:, span])
        if partial is not None:
            coupled = partial[...] + coupled
        for ref in outs[PIECES:]:
            ref[...] = coupled
        result = begin[...] - times(coupled, d_high[...], d_low[...])
        for piece in range(PIECES):
            outs[piece][...] = result[piece * width : (piece + 1) * width]


def fetch(now, before, newest, meta, matrices, starts, after):
    tiles, block, _ = matrices[0].shape
    half = starts[0].shape[0]
    bf16 = jnp.bfloat16
    return pl.pallas_call(
        functools.partial(fetch_kernel, now, before, newest, len(after)),
        out_shape=[
            pltpu.VMEM((block, SIDES * block), bf16),
            pltpu.VMEM((block, SIDES * block), bf16),
            pltpu.VMEM((block, block), bf16),
            pltpu.VMEM((block, block), bf16),
            pltpu.VMEM((half, block), jnp.float32),
            pltpu.VMEM((EXTRA, block), jnp.int32),
            pltpu.VMEM((EXTRA, block), jnp.int32),
        ],
        in_specs=[smem()] + [hbm(), anywhere()] * 2 + [vmem()] * 2 + [anywhere()] * len(after),
        out_specs=[vmem()] * 7,
        scratch_shapes=[
            pltpu.VMEM((SIDES + 1, block, block), jnp.float32),
            pltpu.SemaphoreType.DMA((SIDES + 1,)),
        ],
        compiler_params=params(16),
        cost_estimate=pl.CostEstimate(flops=0, bytes_accessed=24 * block * block, transcendentals=0),
        name=f"fetch_{now}_{newest}",
    )(meta, *matrices, *near(starts), *after)


def add_older(now, older, meta, matrices, weights, here, known, base):
    tiles, block, _ = matrices[0].shape
    operands = [piece[side] for c in older for side in range(SIDES) for piece in known[c]]
    operands = near([*weights, *here, *operands, *base])
    counts = [len(here)] + [len(known[c]) for c in older]
    slots = max(1, SIDES * len(older))
    half = sum(piece.shape[0] for piece in here)
    return pl.pallas_call(
        functools.partial(older_kernel, now, older, counts, len(base)),
        out_shape=pltpu.VMEM((half, block), jnp.float32),
        in_specs=[smem(), hbm(), anywhere()] + [vmem()] * len(operands),
        out_specs=vmem(),
        scratch_shapes=[
            pltpu.VMEM((slots, block, block), jnp.float32),
            pltpu.SemaphoreType.DMA((slots,)),
        ],
        compiler_params=params(24),
        cost_estimate=pl.CostEstimate(
            flops=4 * block * block * 128 * slots, bytes_accessed=4 * block * block * slots, transcendentals=0
        ),
        name=f"older_{now}",
    )(meta, *matrices[:2], *operands)


def relax(now, fetched, latest, partial, keep_sum):
    *weights, begin, mask, _ = fetched
    half, block = begin.shape
    sides = ORDER[: SIDES - len(partial)]
    operands = [piece[side] for side in sides for piece in latest]
    operands = near([mask, *weights, begin, *operands, *partial])
    out_shape = [pltpu.VMEM((half // PIECES, block), jnp.float32)] * PIECES
    out_shape += [pltpu.VMEM((half, block), jnp.float32)] * keep_sum
    return pl.pallas_call(
        functools.partial(relax_kernel, len(latest), len(sides)),
        out_shape=out_shape,
        in_specs=[vmem()] * len(operands),
        out_specs=[vmem()] * len(out_shape),
        compiler_params=params(16),
        cost_estimate=pl.CostEstimate(
            flops=16 * block * block * 128, bytes_accessed=16 * block * block, transcendentals=0
        ),
        name=f"relax_{now}",
    )(*operands)


def per_device(residual, inv_diag, coupling_tiles, colour, tile_cols):
    axis = "rows"
    count = lax.axis_size(axis)
    groups = count // COLOURS
    me = lax.axis_index(axis)
    core = (me % 2).reshape(1)
    place = me % COLOURS
    group = me // COLOURS
    block, cols = residual.shape
    half = cols // 2
    tiles = jnp.transpose(coupling_tiles, (1, 0, 2))
    number = tiles.shape[0]

    def flip(value, bit):
        return lax.ppermute(value, axis, [(i, i ^ bit) for i in range(count)])

    def shift(value, by):
        return lax.ppermute(value, axis, [(i, (i + by) % count) for i in range(count)])

    def around(here):
        return [shift(here, COLOURS), here, shift(here, -COLOURS)]

    facts = jnp.concatenate([core, colour, tile_cols[0]])
    keep, send, own_rows = pl.pallas_call(
        first_kernel,
        out_shape=[pltpu.VMEM((half, block), jnp.float32)]
        + [pltpu.VMEM((half + EXTRA, block), jnp.float32), pltpu.VMEM((EXTRA, block), jnp.float32)],
        in_specs=[smem(), hbm(), hbm()],
        out_specs=[vmem()] * 3,
        scratch_shapes=[
            pltpu.VMEM((block, block), jnp.float32),
            pltpu.VMEM((block, cols), jnp.float32),
            pltpu.SemaphoreType.DMA((2,)),
        ],
        compiler_params=params(16),
        name="first",
    )(facts, *far([inv_diag, residual]))
    arrived = flip(send, 1)
    starts = [keep, arrived]
    own_colour = colour[0]
    sib_facts = arrived[half : half + 1 + number, 0].astype(jnp.int32)
    sib_colour = sib_facts[0]

    late_tiles, late_inverse, _ = lax.optimization_barrier((tiles, inv_diag, arrived))
    own_tiles, own_inverse = far([tiles, inv_diag])
    matrices = [own_tiles, flip(late_tiles, 1), own_inverse, flip(late_inverse, 1)]

    own_wide, sib_wide = own_rows[:1], arrived[half : half + 1]
    candidate = jnp.where(own_wide == 0, keep, arrived[:half])
    wheel = lax.broadcasted_iota(jnp.int32, (EXTRA, block), 0).astype(jnp.float32)
    places = jnp.where(wheel == own_wide, place, 0) + jnp.where(wheel == sib_wide, place ^ 1, 0)
    places = places.astype(jnp.float32)
    sent = jnp.concatenate([candidate, places])
    swapped = flip(sent, 2)
    here = jnp.where((own_wide == 0) | (sib_wide == 0), candidate, swapped[:half])
    known = {0: [around(jnp.concatenate([here, places + swapped[half:]]))]}
    blocks = []
    for side in range(SIDES):
        found = known[0][0][side][half : half + COLOURS, 0].astype(jnp.int32)
        blocks.append((((group + side - 1) % groups) * COLOURS + found).astype(jnp.int32))
    meta = jnp.concatenate([colour, sib_facts[:1], tile_cols[0], sib_facts[1:]] + blocks)

    order = list(range(1, COLOURS)) + list(range(COLOURS - 2, -1, -1))
    newest = 0
    sums, used, finals = {}, {}, {}
    fetched, partial = fetch(order[0], 0, 0, meta, matrices, starts, []), []
    for step, now in enumerate(order):
        used[now] = {(c, done_at(order, c, step)) for c in known if c != now}
        outs = relax(now, fetched, known[newest], partial, int(now in order[step + 1 :]))
        candidates, sums[now] = outs[:PIECES], outs[PIECES:]
        finals[now] = candidates
        if step == len(order) - 1:
            break
        after = order[step + 1]
        swapped = [flip(c, 2) for c in candidates]
        before = fetched[-2]
        fetched = fetch(after, now, now, meta, matrices, starts, candidates)
        masks = [before] * (PIECES - 1) + [fetched[-1]]
        here = [jnp.where(m[:1] != 0, c, s) for m, c, s in zip(masks, candidates, swapped)]
        fresh = used.get(after, set())
        older = tuple(c for c in sorted(known) if c not in (now, after) and (c, done_at(order, c, step)) not in fresh)
        partial = [add_older(after, older, meta, matrices, fetched[:2], here, known, sums.get(after, []))]
        known[now] = [around(h) for h in here]
        newest = now

    own_final, sib_final = finals[0], finals[0]
    for c in range(1, COLOURS):
        own_final = [jnp.where(own_colour == c, a, b) for a, b in zip(finals[c], own_final)]
        sib_final = [jnp.where(sib_colour == c, a, b) for a, b in zip(finals[c], sib_final)]
    mine, other = jnp.concatenate(own_final), flip(jnp.concatenate(sib_final), 1)
    return pl.pallas_call(
        last_kernel,
        out_shape=jax.ShapeDtypeStruct((block, cols), jnp.float32),
        in_specs=[smem(), vmem(), vmem()],
        out_specs=vmem(),
        compiler_params=params(16),
        name="last",
    )(core, *near([mine, other]))


def done_at(order, colour, step):
    return max([i for i in range(step) if order[i] == colour], default=-1)


def solution(mesh):
    in_specs = (P("rows", None), P("rows", None), P("rows", None, None), P("rows"), P("rows", None))
    out_specs = P("rows", None)
    return jax.shard_map(
        per_device, mesh=mesh, in_specs=in_specs, out_specs=out_specs, check_vma=False
    )
```

```python
import functools

import jax
import jax.numpy as jnp
from jax import lax
from jax.experimental import pallas as pl
from jax.experimental.pallas import tpu as pltpu
from jax.sharding import PartitionSpec as P

COLOURS = 4
SIDES = 3
INNER, OUTER, HERE = range(3)
EXTRA = 8
OWN_COLOUR = 0
SIB_COLOUR = 1
TILE_START = 2


def dot_t(a, b):
    return lax.dot_general(a, b, (((1,), (1,)), ((), ())), preferred_element_type=jnp.float32)


def split(value):
    high = value.astype(jnp.bfloat16)
    return high, (value - high.astype(jnp.float32)).astype(jnp.bfloat16)


def times(value, high, low):
    rows = value.shape[0]
    parts = jnp.concatenate(split(value), axis=0)
    product = dot_t(parts, high) + dot_t(parts, low)
    return product[:rows] + product[rows:]


def vmem():
    return pl.BlockSpec(memory_space=pltpu.VMEM)


def smem():
    return pl.BlockSpec(memory_space=pltpu.SMEM)


def anywhere():
    return pl.BlockSpec(memory_space=pl.ANY)


def hbm():
    return pl.BlockSpec(memory_space=pltpu.HBM)


def params(mebibytes):
    return pltpu.CompilerParams(vmem_limit_bytes=mebibytes * 1024 * 1024)


def far(values):
    return [pltpu.with_memory_space_constraint(v, pltpu.HBM) for v in values]


def near(values):
    return [pltpu.with_memory_space_constraint(v, pltpu.VMEM) for v in values]


def first_kernel(facts_ref, inverse_hbm, residual_hbm, keep_ref, send_ref, facts_out, inverse_ref, residual_ref, sems):
    copies = [
        pltpu.make_async_copy(residual_hbm, residual_ref, sems.at[0]),
        pltpu.make_async_copy(inverse_hbm, inverse_ref, sems.at[1]),
    ]
    for copy in copies:
        copy.start()
    for copy in copies:
        copy.wait()
    value = times(jnp.transpose(residual_ref[...]), *split(inverse_ref[...]))
    half, block = keep_ref.shape
    is_first = facts_ref[0] == 0
    keep_ref[...] = jnp.where(is_first, value[:half], value[half:])
    send_ref[:half, :] = jnp.where(is_first, value[half:], value[:half])
    row = lax.broadcasted_iota(jnp.int32, (EXTRA, block), 0)
    rows = jnp.zeros((EXTRA, block), jnp.int32)
    for i in range(1, facts_ref.shape[0]):
        rows = jnp.where(row == i - 1, facts_ref[i], rows)
    send_ref[half:, :] = rows.astype(jnp.float32)
    facts_out[...] = rows.astype(jnp.float32)


def last_kernel(core_ref, mine_ref, other_ref, out_ref):
    is_first = core_ref[0] == 0
    mine, other = mine_ref[...], other_ref[...]
    first = jnp.where(is_first, mine, other)
    second = jnp.where(is_first, other, mine)
    out_ref[...] = jnp.transpose(jnp.concatenate([first, second], axis=0))


def tile_of(meta_ref, own, tiles, colour, side):
    wanted = meta_ref[TILE_START + 2 * tiles + side * COLOURS + colour]
    start = jnp.where(own, TILE_START, TILE_START + tiles)
    found = jnp.int32(-1)
    for k in range(tiles):
        found = jnp.where(meta_ref[start + k] == wanted, k, found)
    return found


def mover(own, own_src, sib_src, dst, sem):
    def move(act):
        for is_own, src in ((own, own_src), (jnp.logical_not(own), sib_src)):
            @pl.when(is_own)
            def _(src=src):
                act(pltpu.make_async_copy(src, dst, sem))

    return move


def start(copy):
    copy.start()


def wait(copy):
    copy.wait()


def is_active(meta_ref, now):
    return (meta_ref[OWN_COLOUR] == now) | (meta_ref[SIB_COLOUR] == now)


def fetch_kernel(now, before, newest, n_after, meta_ref, own_tiles, sib_tiles, own_inverse, sib_inverse, own_start, sib_start, *refs):
    w_high, w_low, d_high, d_low, begin, mask, mask_before, buffer, sems = refs[n_after:]
    tiles, block = own_tiles.shape[0], own_tiles.shape[1]
    half = begin.shape[0]
    own = meta_ref[OWN_COLOUR] == now
    active = is_active(meta_ref, now)
    mask[...] = jnp.broadcast_to(active.astype(jnp.int32), mask.shape)
    mask_before[...] = jnp.broadcast_to(is_active(meta_ref, before).astype(jnp.int32), mask.shape)

    @pl.when(active)
    def _():
        which = [tile_of(meta_ref, own, tiles, newest, side) for side in range(SIDES)]
        moves = [mover(own, own_tiles.at[k], sib_tiles.at[k], buffer.at[i], sems.at[i]) for i, k in enumerate(which)]
        moves.append(mover(own, own_inverse, sib_inverse, buffer.at[SIDES], sems.at[SIDES]))
        moves[-1](start)
        for k, move in zip(which, moves):
            @pl.when(k >= 0)
            def _():
                move(start)

        begin[...] = jnp.where(own, own_start[...], sib_start[:half, :])
        moves[-1](wait)
        d_high[...], d_low[...] = split(buffer[SIDES])
        for i, k in enumerate(which):
            span = pl.ds(i * block, block)

            @pl.when(k >= 0)
            def _():
                moves[i](wait)
                w_high[:, span], w_low[:, span] = split(buffer[i])

            @pl.when(k < 0)
            def _():
                w_high[:, span] = jnp.zeros((block, block), jnp.bfloat16)
                w_low[:, span] = jnp.zeros((block, block), jnp.bfloat16)


def older_kernel(now, older, has_base, meta_ref, own_tiles, sib_tiles, w_high, w_low, outer, here, *refs):
    *refs, partial, buffer, sems = refs
    known, base = refs[: SIDES * len(older)], refs[SIDES * len(older) :]
    tiles, block = own_tiles.shape[0], own_tiles.shape[1]
    half = partial.shape[0]
    own = meta_ref[OWN_COLOUR] == now

    @pl.when(is_active(meta_ref, now))
    def _():
        which = [tile_of(meta_ref, own, tiles, c, side) for c in older for side in range(SIDES)]
        moves = [mover(own, own_tiles.at[k], sib_tiles.at[k], buffer.at[i], sems.at[i]) for i, k in enumerate(which)]
        for k, move in zip(which, moves):
            @pl.when(k >= 0)
            def _():
                move(start)

        span = pl.ds(OUTER * block, 2 * block)
        newest = jnp.concatenate([outer[:half, :], here[:half, :]], axis=1)
        total = times(newest, w_high[:, span], w_low[:, span])
        partial[...] = base[0][...] + total if has_base else total
        for i, k in enumerate(which):
            @pl.when(k >= 0)
            def _():
                moves[i](wait)
                partial[...] += times(known[i][:half, :], *split(buffer[i]))


def relax_kernel(sides, mask, w_high, w_low, d_high, d_low, begin, *refs):
    latest, refs = refs[:sides], refs[sides:]
    if sides < SIDES:
        partial, out, *total = refs
    else:
        partial, out, *total = None, *refs
    half, block = begin.shape
    active = mask[0, 0] != 0

    @pl.when(active)
    def _():
        span = pl.ds(0, sides * block)
        values = jnp.concatenate([ref[:half, :] for ref in latest], axis=1)
        coupled = times(values, w_high[:, span], w_low[:, span])
        if partial is not None:
            coupled = partial[...] + coupled
        for ref in total:
            ref[...] = coupled
        out[...] = begin[...] - times(coupled, d_high[...], d_low[...])

    @pl.when(jnp.logical_not(active))
    def _():
        out[...] = jnp.zeros_like(out)


def fetch(now, before, newest, meta, matrices, starts, after):
    tiles, block, _ = matrices[0].shape
    half = starts[0].shape[0]
    bf16 = jnp.bfloat16
    return pl.pallas_call(
        functools.partial(fetch_kernel, now, before, newest, len(after)),
        out_shape=[
            pltpu.VMEM((block, SIDES * block), bf16),
            pltpu.VMEM((block, SIDES * block), bf16),
            pltpu.VMEM((block, block), bf16),
            pltpu.VMEM((block, block), bf16),
            pltpu.VMEM((half, block), jnp.float32),
            pltpu.VMEM((EXTRA, block), jnp.int32),
            pltpu.VMEM((EXTRA, block), jnp.int32),
        ],
        in_specs=[smem()] + [hbm(), anywhere()] * 2 + [vmem()] * 2 + [anywhere()] * len(after),
        out_specs=[vmem()] * 7,
        scratch_shapes=[
            pltpu.VMEM((SIDES + 1, block, block), jnp.float32),
            pltpu.SemaphoreType.DMA((SIDES + 1,)),
        ],
        compiler_params=params(16),
        cost_estimate=pl.CostEstimate(flops=0, bytes_accessed=24 * block * block, transcendentals=0),
        name=f"fetch_{now}_{newest}",
    )(meta, *matrices, *near(starts), *after)


def add_older(now, older, meta, matrices, weights, outer, here, known, base):
    tiles, block, _ = matrices[0].shape
    operands = [value for c in older for value in known[c]]
    operands = near([*weights, outer, here, *operands, *base])
    slots = max(1, SIDES * len(older))
    half = here.shape[0]
    return pl.pallas_call(
        functools.partial(older_kernel, now, older, len(base)),
        out_shape=pltpu.VMEM((half, block), jnp.float32),
        in_specs=[smem(), hbm(), anywhere()] + [vmem()] * len(operands),
        out_specs=vmem(),
        scratch_shapes=[
            pltpu.VMEM((slots, block, block), jnp.float32),
            pltpu.SemaphoreType.DMA((slots,)),
        ],
        compiler_params=params(24),
        cost_estimate=pl.CostEstimate(
            flops=4 * block * block * 128 * slots, bytes_accessed=4 * block * block * slots, transcendentals=0
        ),
        name=f"older_{now}",
    )(meta, *matrices[:2], *operands)


def relax(now, fetched, latest, partial, keep_sum):
    *weights, begin, mask, _ = fetched
    half, block = begin.shape
    sides = 1 if partial else SIDES
    operands = near([mask, *weights, begin, *latest[:sides], *partial])
    out_shape = [pltpu.VMEM((half, block), jnp.float32)] * (1 + keep_sum)
    return pl.pallas_call(
        functools.partial(relax_kernel, sides),
        out_shape=out_shape,
        in_specs=[vmem()] * len(operands),
        out_specs=[vmem()] * len(out_shape),
        compiler_params=params(16),
        cost_estimate=pl.CostEstimate(
            flops=16 * block * block * 128, bytes_accessed=16 * block * block, transcendentals=0
        ),
        name=f"relax_{now}",
    )(*operands)


def per_device(residual, inv_diag, coupling_tiles, colour, tile_cols):
    axis = "rows"
    count = lax.axis_size(axis)
    groups = count // COLOURS
    me = lax.axis_index(axis)
    core = (me % 2).reshape(1)
    place = me % COLOURS
    group = me // COLOURS
    block, cols = residual.shape
    half = cols // 2
    tiles = jnp.transpose(coupling_tiles, (1, 0, 2))
    number = tiles.shape[0]

    def flip(value, bit):
        return lax.ppermute(value, axis, [(i, i ^ bit) for i in range(count)])

    def beside(value, ahead):
        pairs = []
        for i in range(count):
            step = COLOURS if (i // 2) % 2 == ahead else -COLOURS
            pairs.append((i, (i + step) % count))
        return lax.ppermute(value, axis, pairs)

    facts = jnp.concatenate([core, colour, tile_cols[0]])
    keep, send, own_rows = pl.pallas_call(
        first_kernel,
        out_shape=[pltpu.VMEM((half, block), jnp.float32)]
        + [pltpu.VMEM((half + EXTRA, block), jnp.float32), pltpu.VMEM((EXTRA, block), jnp.float32)],
        in_specs=[smem(), hbm(), hbm()],
        out_specs=[vmem()] * 3,
        scratch_shapes=[
            pltpu.VMEM((block, block), jnp.float32),
            pltpu.VMEM((block, cols), jnp.float32),
            pltpu.SemaphoreType.DMA((2,)),
        ],
        compiler_params=params(16),
        name="first",
    )(facts, *far([inv_diag, residual]))
    arrived = flip(send, 1)
    starts = [keep, arrived]
    sib_facts = arrived[half : half + 1 + number, 0].astype(jnp.int32)

    late_tiles, late_inverse, _ = lax.optimization_barrier((tiles, inv_diag, arrived))
    own_tiles, own_inverse = far([tiles, inv_diag])
    matrices = [own_tiles, flip(late_tiles, 1), own_inverse, flip(late_inverse, 1)]

    own_wide, sib_wide = own_rows[:1], arrived[half : half + 1]
    candidate = jnp.where(own_wide == 0, keep, arrived[:half])
    wheel = lax.broadcasted_iota(jnp.int32, (EXTRA, block), 0).astype(jnp.float32)
    places = jnp.where(wheel == own_wide, place + 1, 0) + jnp.where(wheel == sib_wide, (place ^ 1) + 1, 0)
    places = places.astype(jnp.float32)
    sent = jnp.concatenate([candidate, places])
    swapped = flip(sent, 2)
    outer = beside(sent, 1)
    here = jnp.where((own_wide == 0) | (sib_wide == 0), candidate, swapped[:half])
    here = jnp.concatenate([here, places + swapped[half:]])
    known = {0: [beside(here, 0), outer, here]}
    toward = jnp.where(place < COLOURS // 2, -1, 1)
    blocks = []
    for value, step in zip(known[0], (toward, -toward, 0)):
        found = value[half : half + COLOURS, 0].astype(jnp.int32)
        first = ((group + step) % groups) * COLOURS
        blocks.append(jnp.where(found > 0, first + found - 1, -1).astype(jnp.int32))
    meta = jnp.concatenate([colour, sib_facts[:1], tile_cols[0], sib_facts[1:]] + blocks)

    order = list(range(1, COLOURS)) + list(range(COLOURS - 2, -1, -1))
    newest = 0
    sums, used, finals = {}, {}, {}
    fetched, partial = fetch(order[0], 0, 0, meta, matrices, starts, []), []
    for step, now in enumerate(order):
        used[now] = {(c, done_at(order, c, step)) for c in known if c != now}
        outs = relax(now, fetched, known[newest], partial, int(now in order[step + 1 :]))
        candidate, sums[now] = outs[0], outs[1:]
        finals[now] = candidate
        if step == len(order) - 1:
            break
        after = order[step + 1]
        swapped = flip(candidate, 2)
        outer = beside(candidate, 1)
        fetched = fetch(after, now, now, meta, matrices, starts, [candidate])
        here = jnp.where(fetched[-1][:1] != 0, candidate, swapped)
        inner = beside(here, 0)
        fresh = used.get(after, set())
        older = tuple(c for c in sorted(known) if c not in (now, after) and (c, done_at(order, c, step)) not in fresh)
        partial = [add_older(after, older, meta, matrices, fetched[:2], outer, here, known, sums.get(after, []))]
        known[now] = [inner, outer, here]
        newest = now

    own_final, sib_final = finals[0], finals[0]
    for c in range(1, COLOURS):
        own_final = jnp.where(own_wide == c, finals[c], own_final)
        sib_final = jnp.where(sib_wide == c, finals[c], sib_final)
    mine, other = own_final, flip(sib_final, 1)
    return pl.pallas_call(
        last_kernel,
        out_shape=jax.ShapeDtypeStruct((block, cols), jnp.float32),
        in_specs=[smem(), vmem(), vmem()],
        out_specs=vmem(),
        compiler_params=params(16),
        name="last",
    )(core, *near([mine, other]))


def done_at(order, colour, step):
    return max([i for i in range(step) if order[i] == colour], default=-1)


def solution(mesh):
    in_specs = (P("rows", None), P("rows", None), P("rows", None, None), P("rows"), P("rows", None))
    out_specs = P("rows", None)
    return jax.shard_map(
        per_device, mesh=mesh, in_specs=in_specs, out_specs=out_specs, check_vma=False
    )
```

```python
import functools

import jax
import jax.numpy as jnp
from jax import lax
from jax.experimental import pallas as pl
from jax.experimental.pallas import tpu as pltpu
from jax.sharding import PartitionSpec as P

COLOURS = 4
SIDES = 3
INNER, OUTER, HERE = range(3)
EXTRA = 8
LANES = 128
ACTIVE, IS_OWN, TILE = range(3)


def dot_t(a, b):
    return lax.dot_general(a, b, (((1,), (1,)), ((), ())), preferred_element_type=jnp.float32)


def split(value):
    high = value.astype(jnp.bfloat16)
    return high, (value - high.astype(jnp.float32)).astype(jnp.bfloat16)


def times(value, high, low):
    rows = value.shape[0]
    parts = jnp.concatenate(split(value), axis=0)
    product = dot_t(parts, high) + dot_t(parts, low)
    return product[:rows] + product[rows:]


def vmem():
    return pl.BlockSpec(memory_space=pltpu.VMEM)


def smem():
    return pl.BlockSpec(memory_space=pltpu.SMEM)


def anywhere():
    return pl.BlockSpec(memory_space=pl.ANY)


def hbm():
    return pl.BlockSpec(memory_space=pltpu.HBM)


def params(mebibytes):
    return pltpu.CompilerParams(vmem_limit_bytes=mebibytes * 1024 * 1024)


def far(values):
    return [pltpu.with_memory_space_constraint(v, pltpu.HBM) for v in values]


def near(values):
    return [pltpu.with_memory_space_constraint(v, pltpu.VMEM) for v in values]


def first_kernel(core_ref, colour_ref, tile_cols_ref, inverse_hbm, residual_hbm, keep_ref, send_ref, facts_out, inverse_ref, residual_ref, sems):
    copies = [
        pltpu.make_async_copy(residual_hbm, residual_ref, sems.at[0]),
        pltpu.make_async_copy(inverse_hbm, inverse_ref, sems.at[1]),
    ]
    for copy in copies:
        copy.start()
    for copy in copies:
        copy.wait()
    value = times(jnp.transpose(residual_ref[...]), *split(inverse_ref[...]))
    half, block = keep_ref.shape
    is_first = core_ref[0] == 0
    keep_ref[...] = jnp.where(is_first, value[:half], value[half:])
    send_ref[:half, :] = jnp.where(is_first, value[half:], value[:half])
    row = lax.broadcasted_iota(jnp.int32, (EXTRA, block), 0)
    rows = jnp.where(row == 0, colour_ref[0], 0)
    for k in range(tile_cols_ref.shape[1]):
        rows = jnp.where(row == k + 1, tile_cols_ref[0, k], rows)
    send_ref[half:, :] = rows.astype(jnp.float32)
    facts_out[...] = rows.astype(jnp.float32)


def last_kernel(core_ref, mine_ref, other_ref, out_ref):
    is_first = core_ref[0] == 0
    mine, other = mine_ref[...], other_ref[...]
    first = jnp.where(is_first, mine, other)
    second = jnp.where(is_first, other, mine)
    out_ref[...] = jnp.transpose(jnp.concatenate([first, second], axis=0))


def parts_kernel(tiles_ref, inverse_ref, w_high, w_low, zeros, buffer, sems):
    zeros[...] = jnp.zeros_like(zeros)
    tiles = tiles_ref.shape[0]
    copies = [pltpu.make_async_copy(tiles_ref.at[k], buffer.at[k], sems.at[k]) for k in range(tiles)]
    copies.append(pltpu.make_async_copy(inverse_ref, buffer.at[tiles], sems.at[tiles]))
    for copy in copies:
        copy.start()
    for k, copy in enumerate(copies):
        copy.wait()
        w_high[k], w_low[k] = split(buffer[k])


def plan_kernel(tiles, firsts_ref, _, own_rows, arrived, inner, outer, here, *outs):
    half = arrived.shape[0] - EXTRA
    lanes = pl.ds(0, LANES)
    own = own_rows[:, lanes].astype(jnp.int32)
    sib = arrived[half:, lanes].astype(jnp.int32)
    wanted = []
    for side, ref in enumerate((inner, outer, here)):
        found = ref[half:, lanes].astype(jnp.int32)
        wanted.append(jnp.where(found > 0, firsts_ref[side] + found - 1, -1))
    rows = outs[0].shape[0]
    row = lax.broadcasted_iota(jnp.int32, (rows, LANES), 0)
    for now in range(COLOURS):
        is_own, is_sib = own[:1] == now, sib[:1] == now
        active = (is_own | is_sib).astype(jnp.int32)
        plan = jnp.where(row == ACTIVE, active, is_own.astype(jnp.int32))
        listed = [jnp.where(is_own, own[k + 1 : k + 2], sib[k + 1 : k + 2]) for k in range(tiles)]
        for side in range(SIDES):
            found = jnp.full((EXTRA, LANES), -1, jnp.int32)
            for k in range(tiles):
                found = jnp.where(wanted[side] == listed[k], k, found)
            for c in range(COLOURS):
                plan = jnp.where(row == TILE + side * COLOURS + c, found[c : c + 1], plan)
        outs[now][...] = plan
        mask = outs[COLOURS + now]
        mask[...] = jnp.concatenate([jnp.broadcast_to(active, (EXTRA, LANES))] * (mask.shape[1] // LANES), axis=1)


def chosen(plan, body, own, sib):
    active, is_own = plan[ACTIVE, 0] != 0, plan[IS_OWN, 0] != 0

    @pl.when(active & is_own)
    def _():
        body(*own)

    @pl.when(active & jnp.logical_not(is_own))
    def _():
        body(*sib)


def older_kernel(newest, older, has_base, plan, own_high, own_low, sib_high, sib_low, outer, here, *refs):
    *refs, partial = refs
    known, base = refs[: SIDES * len(older)], refs[SIDES * len(older) :]
    half = partial.shape[0]
    slots = [(newest, OUTER, outer), (newest, HERE, here)]
    slots += [(c, side, known[SIDES * i + side]) for i, c in enumerate(older) for side in range(SIDES)]

    def body(w_high, w_low):
        partial[...] = base[0][...] if has_base else jnp.zeros_like(partial)
        for c, side, ref in slots:
            k = plan[TILE + side * COLOURS + c, 0]

            @pl.when(k >= 0)
            def _():
                partial[...] += times(ref[:half, :], w_high[k], w_low[k])

    chosen(plan, body, (own_high, own_low), (sib_high, sib_low))


def relax_kernel(newest, sides, plan, own_high, own_low, sib_high, sib_low, own_start, sib_start, *refs):
    latest, refs = refs[:sides], refs[sides:]
    base, refs = refs[: int(sides < SIDES)], refs[int(sides < SIDES) :]
    out, total = refs[:2]
    half = out.shape[0]

    def body(w_high, w_low, begin):
        total[...] = base[0][...] if base else jnp.zeros_like(total)
        for side, ref in enumerate(latest):
            k = plan[TILE + side * COLOURS + newest, 0]

            @pl.when(k >= 0)
            def _():
                total[...] += times(ref[:half, :], w_high[k], w_low[k])

        last = w_high.shape[0] - 1
        out[...] = begin[:half, :] - times(total[...], w_high[last], w_low[last])

    chosen(plan, body, (own_high, own_low, own_start), (sib_high, sib_low, sib_start))

    @pl.when(plan[ACTIVE, 0] == 0)
    def _():
        out[...] = jnp.zeros_like(out)


def parts(tiles, inverse, name):
    count, block, _ = tiles.shape
    return pl.pallas_call(
        parts_kernel,
        out_shape=[pltpu.VMEM((count + 1, block, block), jnp.bfloat16)] * 2 + [pltpu.VMEM((EXTRA, block), jnp.float32)],
        in_specs=[anywhere()] * 2,
        out_specs=[vmem()] * 3,
        scratch_shapes=[
            pltpu.VMEM((count + 1, block, block), jnp.float32),
            pltpu.SemaphoreType.DMA((count + 1,)),
        ],
        compiler_params=params(12),
        cost_estimate=pl.CostEstimate(flops=0, bytes_accessed=8 * count * block * block, transcendentals=0),
        name=name,
    )(tiles, inverse)


def make_plans(tiles, firsts, own_rows, arrived, first_known, zeros):
    block = own_rows.shape[1]
    rows = -(-(TILE + SIDES * COLOURS) // EXTRA) * EXTRA
    outs = pl.pallas_call(
        functools.partial(plan_kernel, tiles),
        out_shape=[pltpu.VMEM((rows, LANES), jnp.int32)] * COLOURS + [pltpu.VMEM((EXTRA, block), jnp.int32)] * COLOURS,
        in_specs=[smem()] + [vmem()] * 6,
        out_specs=[vmem()] * (2 * COLOURS),
        compiler_params=params(8),
        name="plan",
    )(firsts, *near([zeros, own_rows, arrived, *first_known]))
    return outs[:COLOURS], outs[COLOURS:]


def add_older(now, newest, older, plan, matrices, outer, here, known, base):
    half, block = here.shape
    operands = near([plan, *matrices, outer, here, *[value for c in older for value in known[c]], *base])
    slots = 2 + SIDES * len(older)
    return pl.pallas_call(
        functools.partial(older_kernel, newest, older, len(base)),
        out_shape=pltpu.VMEM((half, block), jnp.float32),
        in_specs=[vmem()] * len(operands),
        out_specs=vmem(),
        compiler_params=params(8),
        cost_estimate=pl.CostEstimate(
            flops=4 * block * block * LANES * slots, bytes_accessed=4 * block * block * slots, transcendentals=0
        ),
        name=f"older_{now}",
    )(*operands)


def relax(now, newest, plan, matrices, starts, latest, partial, keep_sum):
    half, block = starts[0].shape
    sides = 1 if partial else SIDES
    operands = near([plan, *matrices, *starts, *latest[:sides], *partial])
    value = pltpu.VMEM((half, block), jnp.float32)
    return pl.pallas_call(
        functools.partial(relax_kernel, newest, sides),
        out_shape=[value] * (1 + keep_sum),
        in_specs=[vmem()] * len(operands),
        out_specs=[vmem()] * (1 + keep_sum),
        scratch_shapes=[value] * (1 - keep_sum),
        compiler_params=params(8),
        cost_estimate=pl.CostEstimate(
            flops=16 * block * block * LANES, bytes_accessed=16 * block * block, transcendentals=0
        ),
        name=f"relax_{now}",
    )(*operands)


def per_device(residual, inv_diag, coupling_tiles, colour, tile_cols):
    axis = "rows"
    count = lax.axis_size(axis)
    groups = count // COLOURS
    me = lax.axis_index(axis)
    core = (me % 2).reshape(1)
    place = me % COLOURS
    group = me // COLOURS
    block, cols = residual.shape
    half = cols // 2
    tiles = jnp.transpose(coupling_tiles, (1, 0, 2))
    number = tiles.shape[0]

    def flip(value, bit):
        return lax.ppermute(value, axis, [(i, i ^ bit) for i in range(count)])

    def beside(value, ahead):
        pairs = []
        for i in range(count):
            step = COLOURS if (i // 2) % 2 == ahead else -COLOURS
            pairs.append((i, (i + step) % count))
        return lax.ppermute(value, axis, pairs)

    keep, send, own_rows = pl.pallas_call(
        first_kernel,
        out_shape=[pltpu.VMEM((half, block), jnp.float32)]
        + [pltpu.VMEM((half + EXTRA, block), jnp.float32), pltpu.VMEM((EXTRA, block), jnp.float32)],
        in_specs=[smem(), smem(), smem(), hbm(), hbm()],
        out_specs=[vmem()] * 3,
        scratch_shapes=[
            pltpu.VMEM((block, block), jnp.float32),
            pltpu.VMEM((block, cols), jnp.float32),
            pltpu.SemaphoreType.DMA((2,)),
        ],
        compiler_params=params(16),
        name="first",
    )(core, colour, tile_cols, *far([inv_diag, residual]))
    arrived = flip(send, 1)
    starts = [keep, arrived]

    late_tiles, late_inverse, _ = lax.optimization_barrier((tiles, inv_diag, arrived))
    sib_tiles, sib_inverse = flip(late_tiles, 1), flip(late_inverse, 1)

    own_wide, sib_wide = own_rows[:1], arrived[half : half + 1]
    candidate = jnp.where(own_wide == 0, keep, arrived[:half])
    wheel = lax.broadcasted_iota(jnp.int32, (EXTRA, block), 0).astype(jnp.float32)
    places = jnp.where(wheel == own_wide, place + 1, 0) + jnp.where(wheel == sib_wide, (place ^ 1) + 1, 0)
    places = places.astype(jnp.float32)
    sent = jnp.concatenate([candidate, places])
    swapped = flip(sent, 2)
    outer = beside(sent, 1)
    far_tiles, far_inverse, _ = lax.optimization_barrier((tiles, inv_diag, sent))
    *own_parts, zeros = parts(*far([far_tiles, far_inverse]), "own_parts")
    here = jnp.where((own_wide + zeros[:1] == 0) | (sib_wide == 0), candidate, swapped[:half])
    here = jnp.concatenate([here, places + swapped[half:]])
    known = {0: [beside(here, 0), outer, here]}
    toward = jnp.where(place < COLOURS // 2, -1, 1)
    firsts = jnp.stack([((group + step) % groups) * COLOURS for step in (toward, -toward, 0 * toward)]).astype(jnp.int32)
    *sib_parts, zeros = parts(sib_tiles, sib_inverse, "sib_parts")
    matrices = [*own_parts, *sib_parts]
    plans, masks = make_plans(number, firsts, own_rows, arrived, known[0], zeros)

    order = list(range(1, COLOURS)) + list(range(COLOURS - 2, -1, -1))
    newest = 0
    sums, used, finals = {}, {}, {}
    partial = []
    for step, now in enumerate(order):
        used[now] = {(c, done_at(order, c, step)) for c in known if c != now}
        outs = relax(now, newest, plans[now], matrices, starts, known[newest], partial, int(now in order[step + 1 :]))
        candidate, sums[now] = outs[0], outs[1:]
        finals[now] = candidate
        if step == len(order) - 1:
            break
        after = order[step + 1]
        swapped = flip(candidate, 2)
        outer = beside(candidate, 1)
        here = jnp.where(masks[now][:1] != 0, candidate, swapped)
        inner = beside(here, 0)
        fresh = used.get(after, set())
        older = tuple(c for c in sorted(known) if c not in (now, after) and (c, done_at(order, c, step)) not in fresh)
        partial = [add_older(after, now, older, plans[after], matrices, outer, here, known, sums.get(after, []))]
        known[now] = [inner, outer, here]
        newest = now

    own_final, sib_final = finals[0], finals[0]
    for c in range(1, COLOURS):
        own_final = jnp.where(own_wide == c, finals[c], own_final)
        sib_final = jnp.where(sib_wide == c, finals[c], sib_final)
    mine, other = own_final, flip(sib_final, 1)
    return pl.pallas_call(
        last_kernel,
        out_shape=jax.ShapeDtypeStruct((block, cols), jnp.float32),
        in_specs=[smem(), vmem(), vmem()],
        out_specs=vmem(),
        compiler_params=params(16),
        name="last",
    )(core, *near([mine, other]))


def done_at(order, colour, step):
    return max([i for i in range(step) if order[i] == colour], default=-1)


def solution(mesh):
    in_specs = (P("rows", None), P("rows", None), P("rows", None, None), P("rows"), P("rows", None))
    out_specs = P("rows", None)
    return jax.shard_map(
        per_device, mesh=mesh, in_specs=in_specs, out_specs=out_specs, check_vma=False
    )
```

```python
import functools

import jax
import jax.numpy as jnp
from jax import lax
from jax.experimental import pallas as pl
from jax.experimental.pallas import tpu as pltpu
from jax.sharding import PartitionSpec as P

COLOURS = 4
SIDES = 3
INNER, OUTER, HERE = range(3)
EXTRA = 8
LANES = 128
ACTIVE, IS_OWN, TILE = range(3)


def dot_t(a, b):
    return lax.dot_general(a, b, (((1,), (1,)), ((), ())), preferred_element_type=jnp.float32)


def split(value):
    high = value.astype(jnp.bfloat16)
    return high, (value - high.astype(jnp.float32)).astype(jnp.bfloat16)


def times(value, high, low):
    rows = value.shape[0]
    parts = jnp.concatenate(split(value), axis=0)
    product = dot_t(parts, high) + dot_t(parts, low)
    return product[:rows] + product[rows:]


def vmem():
    return pl.BlockSpec(memory_space=pltpu.VMEM)


def smem():
    return pl.BlockSpec(memory_space=pltpu.SMEM)


def anywhere():
    return pl.BlockSpec(memory_space=pl.ANY)


def hbm():
    return pl.BlockSpec(memory_space=pltpu.HBM)


def params(mebibytes):
    return pltpu.CompilerParams(vmem_limit_bytes=mebibytes * 1024 * 1024)


def far(values):
    return [pltpu.with_memory_space_constraint(v, pltpu.HBM) for v in values]


def near(values):
    return [pltpu.with_memory_space_constraint(v, pltpu.VMEM) for v in values]


def first_kernel(core_ref, colour_ref, tile_cols_ref, inverse_hbm, residual_hbm, keep_ref, send_ref, facts_out, inverse_ref, residual_ref, sems):
    copies = [
        pltpu.make_async_copy(residual_hbm, residual_ref, sems.at[0]),
        pltpu.make_async_copy(inverse_hbm, inverse_ref, sems.at[1]),
    ]
    for copy in copies:
        copy.start()
    for copy in copies:
        copy.wait()
    value = times(jnp.transpose(residual_ref[...]), *split(inverse_ref[...]))
    half, block = keep_ref.shape
    is_first = core_ref[0] == 0
    keep_ref[...] = jnp.where(is_first, value[:half], value[half:])
    send_ref[:half, :] = jnp.where(is_first, value[half:], value[:half])
    row = lax.broadcasted_iota(jnp.int32, (EXTRA, block), 0)
    rows = jnp.where(row == 0, colour_ref[0], 0)
    for k in range(tile_cols_ref.shape[1]):
        rows = jnp.where(row == k + 1, tile_cols_ref[0, k], rows)
    send_ref[half:, :] = rows.astype(jnp.float32)
    facts_out[...] = rows.astype(jnp.float32)


def last_kernel(core_ref, mine_ref, other_ref, out_ref):
    is_first = core_ref[0] == 0
    mine, other = mine_ref[...], other_ref[...]
    first = jnp.where(is_first, mine, other)
    second = jnp.where(is_first, other, mine)
    out_ref[...] = jnp.transpose(jnp.concatenate([first, second], axis=0))


def parts_kernel(stored, tiles_ref, inverse_ref, w_high, w_low, zeros, buffer, sems, *held):
    zeros[...] = jnp.zeros_like(zeros)
    tiles = tiles_ref.shape[0]
    copies = [pltpu.make_async_copy(tiles_ref.at[k], buffer.at[k], sems.at[0, k]) for k in range(tiles)]
    copies.append(pltpu.make_async_copy(inverse_ref, buffer.at[tiles], sems.at[0, tiles]))
    for copy in copies:
        copy.start()
    high, low = held if stored else (w_high, w_low)
    stores = []
    for k, copy in enumerate(copies):
        copy.wait()
        high[k], low[k] = split(buffer[k])
        if stored:
            stores.append(pltpu.make_async_copy(high.at[k], w_high.at[k], sems.at[1, k]))
            stores.append(pltpu.make_async_copy(low.at[k], w_low.at[k], sems.at[2, k]))
            stores[-2].start()
            stores[-1].start()
    for store in stores:
        store.wait()


def plan_kernel(tiles, colours, firsts_ref, _, own_rows, arrived, inner, outer, here, *outs):
    half = arrived.shape[0] - EXTRA
    lanes = pl.ds(0, LANES)
    own = own_rows[:, lanes].astype(jnp.int32)
    sib = arrived[half:, lanes].astype(jnp.int32)
    wanted = []
    for side, ref in enumerate((inner, outer, here)):
        found = ref[half:, lanes].astype(jnp.int32)
        wanted.append(jnp.where(found > 0, firsts_ref[side] + found - 1, -1))
    rows = outs[0].shape[0]
    row = lax.broadcasted_iota(jnp.int32, (rows, LANES), 0)
    for i, now in enumerate(colours):
        is_own, is_sib = own[:1] == now, sib[:1] == now
        active = (is_own | is_sib).astype(jnp.int32)
        plan = jnp.where(row == ACTIVE, active, is_own.astype(jnp.int32))
        listed = [jnp.where(is_own, own[k + 1 : k + 2], sib[k + 1 : k + 2]) for k in range(tiles)]
        for side in range(SIDES):
            found = jnp.full((EXTRA, LANES), -1, jnp.int32)
            for k in range(tiles):
                found = jnp.where(wanted[side] == listed[k], k, found)
            for c in range(COLOURS):
                plan = jnp.where(row == TILE + side * COLOURS + c, found[c : c + 1], plan)
        outs[i][...] = plan
        mask = outs[len(colours) + i]
        mask[...] = jnp.concatenate([jnp.broadcast_to(active, (EXTRA, LANES))] * (mask.shape[1] // LANES), axis=1)


def chosen(plan, body, own, sib):
    active, is_own = plan[ACTIVE, 0] != 0, plan[IS_OWN, 0] != 0

    @pl.when(active & is_own)
    def _():
        body(*own)

    @pl.when(active & jnp.logical_not(is_own))
    def _():
        body(*sib)


def older_kernel(newest, older, has_base, plan, own_high, own_low, sib_high, sib_low, outer, here, *refs):
    *refs, partial = refs
    known, base = refs[: SIDES * len(older)], refs[SIDES * len(older) :]
    half = partial.shape[0]
    slots = [(newest, OUTER, outer), (newest, HERE, here)]
    slots += [(c, side, known[SIDES * i + side]) for i, c in enumerate(older) for side in range(SIDES)]

    def body(w_high, w_low):
        partial[...] = base[0][...] if has_base else jnp.zeros_like(partial)
        for c, side, ref in slots:
            k = plan[TILE + side * COLOURS + c, 0]

            @pl.when(k >= 0)
            def _():
                partial[...] += times(ref[:half, :], w_high[k], w_low[k])

    chosen(plan, body, (own_high, own_low), (sib_high, sib_low))


def relax_kernel(newest, sides, plan, own_high, own_low, sib_high, sib_low, own_start, sib_start, *refs):
    latest, refs = refs[:sides], refs[sides:]
    base, refs = refs[: int(sides < SIDES)], refs[int(sides < SIDES) :]
    out, total = refs[:2]
    half = out.shape[0]

    def body(w_high, w_low, begin):
        total[...] = base[0][...] if base else jnp.zeros_like(total)
        for side, ref in enumerate(latest):
            k = plan[TILE + side * COLOURS + newest, 0]

            @pl.when(k >= 0)
            def _():
                total[...] += times(ref[:half, :], w_high[k], w_low[k])

        last = w_high.shape[0] - 1
        out[...] = begin[:half, :] - times(total[...], w_high[last], w_low[last])

    chosen(plan, body, (own_high, own_low, own_start), (sib_high, sib_low, sib_start))

    @pl.when(plan[ACTIVE, 0] == 0)
    def _():
        out[...] = jnp.zeros_like(out)


def parts(tiles, inverse, stored, name):
    count, block, _ = tiles.shape
    shape = (count + 1, block, block)
    space = pltpu.HBM if stored else pltpu.VMEM
    return pl.pallas_call(
        functools.partial(parts_kernel, stored),
        out_shape=[space(shape, jnp.bfloat16)] * 2 + [pltpu.VMEM((EXTRA, block), jnp.float32)],
        in_specs=[anywhere()] * 2,
        out_specs=[hbm() if stored else vmem()] * 2 + [vmem()],
        scratch_shapes=[pltpu.VMEM(shape, jnp.float32), pltpu.SemaphoreType.DMA((3, count + 1))]
        + [pltpu.VMEM(shape, jnp.bfloat16)] * (2 * stored),
        compiler_params=params(20 if stored else 12),
        cost_estimate=pl.CostEstimate(flops=0, bytes_accessed=8 * count * block * block, transcendentals=0),
        name=name,
    )(tiles, inverse)


def make_plans(tiles, colours, firsts, own_rows, arrived, first_known, zeros):
    block = own_rows.shape[1]
    rows = -(-(TILE + SIDES * COLOURS) // EXTRA) * EXTRA
    number = len(colours)
    outs = pl.pallas_call(
        functools.partial(plan_kernel, tiles, colours),
        out_shape=[pltpu.VMEM((rows, LANES), jnp.int32)] * number + [pltpu.VMEM((EXTRA, block), jnp.int32)] * number,
        in_specs=[smem()] + [vmem()] * 6,
        out_specs=[vmem()] * (2 * number),
        compiler_params=params(8),
        name=f"plan_{number}",
    )(firsts, *near([zeros, own_rows, arrived, *first_known]))
    return dict(zip(colours, outs[:number])), dict(zip(colours, outs[number:]))


def add_older(now, newest, older, plan, matrices, outer, here, known, base):
    half, block = here.shape
    operands = near([plan, *matrices, outer, here, *[value for c in older for value in known[c]], *base])
    slots = 2 + SIDES * len(older)
    return pl.pallas_call(
        functools.partial(older_kernel, newest, older, len(base)),
        out_shape=pltpu.VMEM((half, block), jnp.float32),
        in_specs=[vmem()] * len(operands),
        out_specs=vmem(),
        compiler_params=params(8),
        cost_estimate=pl.CostEstimate(
            flops=4 * block * block * LANES * slots, bytes_accessed=4 * block * block * slots, transcendentals=0
        ),
        name=f"older_{now}",
    )(*operands)


def relax(now, newest, plan, matrices, starts, latest, partial, keep_sum):
    half, block = starts[0].shape
    sides = 1 if partial else SIDES
    operands = near([plan, *matrices, *starts, *latest[:sides], *partial])
    value = pltpu.VMEM((half, block), jnp.float32)
    return pl.pallas_call(
        functools.partial(relax_kernel, newest, sides),
        out_shape=[value] * (1 + keep_sum),
        in_specs=[vmem()] * len(operands),
        out_specs=[vmem()] * (1 + keep_sum),
        scratch_shapes=[value] * (1 - keep_sum),
        compiler_params=params(8),
        cost_estimate=pl.CostEstimate(
            flops=16 * block * block * LANES, bytes_accessed=16 * block * block, transcendentals=0
        ),
        name=f"relax_{now}",
    )(*operands)


def per_device(residual, inv_diag, coupling_tiles, colour, tile_cols):
    axis = "rows"
    count = lax.axis_size(axis)
    groups = count // COLOURS
    me = lax.axis_index(axis)
    core = (me % 2).reshape(1)
    place = me % COLOURS
    group = me // COLOURS
    block, cols = residual.shape
    half = cols // 2
    tiles = jnp.transpose(coupling_tiles, (1, 0, 2))
    number = tiles.shape[0]

    def flip(value, bit):
        return lax.ppermute(value, axis, [(i, i ^ bit) for i in range(count)])

    def beside(value, ahead):
        pairs = []
        for i in range(count):
            step = COLOURS if (i // 2) % 2 == ahead else -COLOURS
            pairs.append((i, (i + step) % count))
        return lax.ppermute(value, axis, pairs)

    keep, send, own_rows = pl.pallas_call(
        first_kernel,
        out_shape=[pltpu.VMEM((half, block), jnp.float32)]
        + [pltpu.VMEM((half + EXTRA, block), jnp.float32), pltpu.VMEM((EXTRA, block), jnp.float32)],
        in_specs=[smem(), smem(), smem(), hbm(), hbm()],
        out_specs=[vmem()] * 3,
        scratch_shapes=[
            pltpu.VMEM((block, block), jnp.float32),
            pltpu.VMEM((block, cols), jnp.float32),
            pltpu.SemaphoreType.DMA((2,)),
        ],
        compiler_params=params(16),
        name="first",
    )(core, colour, tile_cols, *far([inv_diag, residual]))
    arrived = flip(send, 1)
    starts = [keep, arrived]

    late_tiles, late_inverse, _ = lax.optimization_barrier((tiles, inv_diag, arrived))
    sib_tiles, sib_inverse = flip(late_tiles, 1), flip(late_inverse, 1)

    own_wide, sib_wide = own_rows[:1], arrived[half : half + 1]
    candidate = jnp.where(own_wide == 0, keep, arrived[:half])
    wheel = lax.broadcasted_iota(jnp.int32, (EXTRA, block), 0).astype(jnp.float32)
    places = jnp.where(wheel == own_wide, place + 1, 0) + jnp.where(wheel == sib_wide, (place ^ 1) + 1, 0)
    places = places.astype(jnp.float32)
    sent = jnp.concatenate([candidate, places])
    swapped = flip(sent, 2)
    outer = beside(sent, 1)
    far_tiles, far_inverse, _ = lax.optimization_barrier((tiles, inv_diag, sent))
    *own_parts, zeros = parts(*far([far_tiles, far_inverse]), 1, "own_parts")
    here = jnp.where((own_wide + zeros[:1] == 0) | (sib_wide == 0), candidate, swapped[:half])
    here = jnp.concatenate([here, places + swapped[half:]])
    known = {0: [beside(here, 0), outer, here]}
    toward = jnp.where(place < COLOURS // 2, -1, 1)
    firsts = jnp.stack([((group + step) % groups) * COLOURS for step in (toward, -toward, 0 * toward)]).astype(jnp.int32)
    *sib_parts, zeros = parts(sib_tiles, sib_inverse, 0, "sib_parts")
    matrices = [*own_parts, *sib_parts]
    facts = (firsts, own_rows, arrived, known[0])
    order = list(range(1, COLOURS)) + list(range(COLOURS - 2, -1, -1))
    plans, masks = make_plans(number, order[:1], *facts, zeros)
    newest = 0
    sums, used, finals = {}, {}, {}
    partial = []
    for step, now in enumerate(order):
        used[now] = {(c, done_at(order, c, step)) for c in known if c != now}
        outs = relax(now, newest, plans[now], matrices, starts, known[newest], partial, int(now in order[step + 1 :]))
        candidate, sums[now] = outs[0], outs[1:]
        finals[now] = candidate
        if step == len(order) - 1:
            break
        if step == 0:
            rest = [c for c in range(COLOURS) if c not in plans]
            for table, more in zip((plans, masks), make_plans(number, rest, *facts, candidate)):
                table.update(more)
        after = order[step + 1]
        swapped = flip(candidate, 2)
        outer = beside(candidate, 1)
        here = jnp.where(masks[now][:1] != 0, candidate, swapped)
        inner = beside(here, 0)
        fresh = used.get(after, set())
        older = tuple(c for c in sorted(known) if c not in (now, after) and (c, done_at(order, c, step)) not in fresh)
        partial = [add_older(after, now, older, plans[after], matrices, outer, here, known, sums.get(after, []))]
        known[now] = [inner, outer, here]
        newest = now

    own_final, sib_final = finals[0], finals[0]
    for c in range(1, COLOURS):
        own_final = jnp.where(own_wide == c, finals[c], own_final)
        sib_final = jnp.where(sib_wide == c, finals[c], sib_final)
    mine, other = own_final, flip(sib_final, 1)
    return pl.pallas_call(
        last_kernel,
        out_shape=jax.ShapeDtypeStruct((block, cols), jnp.float32),
        in_specs=[smem(), vmem(), vmem()],
        out_specs=vmem(),
        compiler_params=params(16),
        name="last",
    )(core, *near([mine, other]))


def done_at(order, colour, step):
    return max([i for i in range(step) if order[i] == colour], default=-1)


def solution(mesh):
    in_specs = (P("rows", None), P("rows", None), P("rows", None, None), P("rows"), P("rows", None))
    out_specs = P("rows", None)
    return jax.shard_map(
        per_device, mesh=mesh, in_specs=in_specs, out_specs=out_specs, check_vma=False
    )
```

```python
import functools

import jax
import jax.numpy as jnp
from jax import lax
from jax.experimental import pallas as pl
from jax.experimental.pallas import tpu as pltpu
from jax.sharding import PartitionSpec as P

COLOURS = 4
SIDES = 3
ARRIVALS = 3
INNER, OUTER, HERE = range(3)
EXTRA = 8
LANES = 128
ACTIVE, IS_OWN, TILE = range(3)


def dot_t(a, b):
    return lax.dot_general(a, b, (((1,), (1,)), ((), ())), preferred_element_type=jnp.float32)


def split(value):
    high = value.astype(jnp.bfloat16)
    return high, (value - high.astype(jnp.float32)).astype(jnp.bfloat16)


def times(value, high, low):
    rows = value.shape[0]
    parts = jnp.concatenate(split(value), axis=0)
    product = dot_t(parts, high) + dot_t(parts, low)
    return product[:rows] + product[rows:]


def vmem():
    return pl.BlockSpec(memory_space=pltpu.VMEM)


def smem():
    return pl.BlockSpec(memory_space=pltpu.SMEM)


def anywhere():
    return pl.BlockSpec(memory_space=pl.ANY)


def hbm():
    return pl.BlockSpec(memory_space=pltpu.HBM)


def params(mebibytes):
    return pltpu.CompilerParams(vmem_limit_bytes=mebibytes * 1024 * 1024)


def far(values):
    return [pltpu.with_memory_space_constraint(v, pltpu.HBM) for v in values]


def near(values):
    return [pltpu.with_memory_space_constraint(v, pltpu.VMEM) for v in values]


def first_kernel(core_ref, colour_ref, tile_cols_ref, inverse_hbm, residual_hbm, keep_ref, send_ref, facts_out, inverse_ref, residual_ref, sems):
    copies = [
        pltpu.make_async_copy(residual_hbm, residual_ref, sems.at[0]),
        pltpu.make_async_copy(inverse_hbm, inverse_ref, sems.at[1]),
    ]
    for copy in copies:
        copy.start()
    for copy in copies:
        copy.wait()
    value = times(jnp.transpose(residual_ref[...]), *split(inverse_ref[...]))
    half, block = keep_ref.shape
    is_first = core_ref[0] == 0
    keep_ref[...] = jnp.where(is_first, value[:half], value[half:])
    send_ref[:half, :] = jnp.where(is_first, value[half:], value[:half])
    row = lax.broadcasted_iota(jnp.int32, (EXTRA, block), 0)
    rows = jnp.where(row == 0, colour_ref[0], 0)
    for k in range(tile_cols_ref.shape[1]):
        rows = jnp.where(row == k + 1, tile_cols_ref[0, k], rows)
    send_ref[half:, :] = rows.astype(jnp.float32)
    facts_out[...] = rows.astype(jnp.float32)


def last_kernel(core_ref, mine_ref, other_ref, out_ref):
    is_first = core_ref[0] == 0
    mine, other = mine_ref[...], other_ref[...]
    first = jnp.where(is_first, mine, other)
    second = jnp.where(is_first, other, mine)
    out_ref[...] = jnp.transpose(jnp.concatenate([first, second], axis=0))


def arrived_inner(inner, rows):
    return sum((ref[rows, :] for ref in inner[1:]), inner[0][rows, :])


def parts_kernel(tiles_ref, inverse_ref, _, w_high, w_low, zeros, buffer, sems):
    zeros[...] = jnp.zeros_like(zeros)
    tiles = tiles_ref.shape[0]
    copies = [pltpu.make_async_copy(tiles_ref.at[k], buffer.at[k], sems.at[k]) for k in range(tiles)]
    copies.append(pltpu.make_async_copy(inverse_ref, buffer.at[tiles], sems.at[tiles]))
    for copy in copies:
        copy.start()
    for k, copy in enumerate(copies):
        copy.wait()
        w_high[k], w_low[k] = split(buffer[k])


def plan_kernel(tiles, colours, firsts_ref, _, own_rows, arrived, *refs):
    inner, (outer, here), outs = refs[:ARRIVALS], refs[ARRIVALS : ARRIVALS + 2], refs[ARRIVALS + 2 :]
    half = arrived.shape[0] - EXTRA
    lanes = pl.ds(0, LANES)
    own = own_rows[:, lanes].astype(jnp.int32)
    sib = arrived[half:, lanes].astype(jnp.int32)
    wanted = []
    rows_of = [arrived_inner(inner, pl.ds(half, EXTRA)), outer[half:, :], here[half:, :]]
    for side, value in enumerate(rows_of):
        found = value[:, :LANES].astype(jnp.int32)
        wanted.append(jnp.where(found > 0, firsts_ref[side] + found - 1, -1))
    rows = outs[0].shape[0]
    row = lax.broadcasted_iota(jnp.int32, (rows, LANES), 0)
    for i, now in enumerate(colours):
        is_own, is_sib = own[:1] == now, sib[:1] == now
        active = (is_own | is_sib).astype(jnp.int32)
        plan = jnp.where(row == ACTIVE, active, is_own.astype(jnp.int32))
        listed = [jnp.where(is_own, own[k + 1 : k + 2], sib[k + 1 : k + 2]) for k in range(tiles)]
        for side in range(SIDES):
            found = jnp.full((EXTRA, LANES), -1, jnp.int32)
            for k in range(tiles):
                found = jnp.where(wanted[side] == listed[k], k, found)
            for c in range(COLOURS):
                plan = jnp.where(row == TILE + side * COLOURS + c, found[c : c + 1], plan)
        outs[i][...] = plan
        mask = outs[len(colours) + i]
        mask[...] = jnp.concatenate([jnp.broadcast_to(active, (EXTRA, LANES))] * (mask.shape[1] // LANES), axis=1)


def chosen(plan, body, own, sib):
    active, is_own = plan[ACTIVE, 0] != 0, plan[IS_OWN, 0] != 0

    @pl.when(active & is_own)
    def _():
        body(*own)

    @pl.when(active & jnp.logical_not(is_own))
    def _():
        body(*sib)


def older_kernel(newest, older, has_base, plan, own_high, own_low, sib_high, sib_low, outer, here, *refs):
    *refs, partial = refs
    each = ARRIVALS + 2
    known, base = refs[: each * len(older)], refs[each * len(older) :]
    half = partial.shape[0]
    slots = [(newest, OUTER, [outer]), (newest, HERE, [here])]
    for i, c in enumerate(older):
        *inner, old_outer, old_here = known[each * i : each * (i + 1)]
        slots += [(c, INNER, inner), (c, OUTER, [old_outer]), (c, HERE, [old_here])]

    def body(w_high, w_low):
        partial[...] = base[0][...] if has_base else jnp.zeros_like(partial)
        for c, side, values in slots:
            k = plan[TILE + side * COLOURS + c, 0]

            @pl.when(k >= 0)
            def _():
                partial[...] += times(arrived_inner(values, pl.ds(0, half)), w_high[k], w_low[k])

    chosen(plan, body, (own_high, own_low), (sib_high, sib_low))


def relax_kernel(newest, sides, plan, own_high, own_low, sib_high, sib_low, own_start, sib_start, *refs):
    inner, refs = refs[:ARRIVALS], refs[ARRIVALS:]
    others, refs = refs[: sides - 1], refs[sides - 1 :]
    base, refs = refs[: int(sides < SIDES)], refs[int(sides < SIDES) :]
    out, total = refs[:2]
    half = out.shape[0]

    def body(w_high, w_low, begin):
        total[...] = base[0][...] if base else jnp.zeros_like(total)
        for side, values in enumerate([inner] + [[ref] for ref in others]):
            k = plan[TILE + side * COLOURS + newest, 0]

            @pl.when(k >= 0)
            def _():
                total[...] += times(arrived_inner(values, pl.ds(0, half)), w_high[k], w_low[k])

        last = w_high.shape[0] - 1
        out[...] = begin[:half, :] - times(total[...], w_high[last], w_low[last])

    chosen(plan, body, (own_high, own_low, own_start), (sib_high, sib_low, sib_start))

    @pl.when(plan[ACTIVE, 0] == 0)
    def _():
        out[...] = jnp.zeros_like(out)


def parts(tiles, inverse, after, name):
    count, block, _ = tiles.shape
    shape = (count + 1, block, block)
    return pl.pallas_call(
        parts_kernel,
        out_shape=[pltpu.VMEM(shape, jnp.bfloat16)] * 2 + [pltpu.VMEM((EXTRA, block), jnp.float32)],
        in_specs=[anywhere()] * 3,
        out_specs=[vmem()] * 3,
        scratch_shapes=[pltpu.VMEM(shape, jnp.float32), pltpu.SemaphoreType.DMA((count + 1,))],
        compiler_params=params(12),
        cost_estimate=pl.CostEstimate(flops=0, bytes_accessed=8 * count * block * block, transcendentals=0),
        name=name,
    )(tiles, inverse, *after)


def flat(sides):
    inner, outer, here = sides
    return [*inner, outer, here]


def make_plans(tiles, colours, firsts, own_rows, arrived, first_known, zeros):
    block = own_rows.shape[1]
    rows = -(-(TILE + SIDES * COLOURS) // EXTRA) * EXTRA
    number = len(colours)
    outs = pl.pallas_call(
        functools.partial(plan_kernel, tiles, colours),
        out_shape=[pltpu.VMEM((rows, LANES), jnp.int32)] * number + [pltpu.VMEM((EXTRA, block), jnp.int32)] * number,
        in_specs=[smem()] + [vmem()] * (5 + ARRIVALS),
        out_specs=[vmem()] * (2 * number),
        compiler_params=params(8),
        name=f"plan_{number}",
    )(firsts, *near([zeros, own_rows, arrived, *flat(first_known)]))
    return dict(zip(colours, outs[:number])), dict(zip(colours, outs[number:]))


def add_older(now, newest, older, plan, matrices, outer, here, known, base):
    half, block = here.shape
    operands = near([plan, *matrices, outer, here, *[value for c in older for value in flat(known[c])], *base])
    slots = 2 + SIDES * len(older)
    return pl.pallas_call(
        functools.partial(older_kernel, newest, older, len(base)),
        out_shape=pltpu.VMEM((half, block), jnp.float32),
        in_specs=[vmem()] * len(operands),
        out_specs=vmem(),
        compiler_params=params(8),
        cost_estimate=pl.CostEstimate(
            flops=4 * block * block * LANES * slots, bytes_accessed=4 * block * block * slots, transcendentals=0
        ),
        name=f"older_{now}",
    )(*operands)


def relax(now, newest, plan, matrices, starts, latest, partial, keep_sum):
    half, block = starts[0].shape
    sides = 1 if partial else SIDES
    operands = near([plan, *matrices, *starts, *flat(latest)[: ARRIVALS - 1 + sides], *partial])
    value = pltpu.VMEM((half, block), jnp.float32)
    return pl.pallas_call(
        functools.partial(relax_kernel, newest, sides),
        out_shape=[value] * (1 + keep_sum),
        in_specs=[vmem()] * len(operands),
        out_specs=[vmem()] * (1 + keep_sum),
        scratch_shapes=[value] * (1 - keep_sum),
        compiler_params=params(8),
        cost_estimate=pl.CostEstimate(
            flops=16 * block * block * LANES, bytes_accessed=16 * block * block, transcendentals=0
        ),
        name=f"relax_{now}",
    )(*operands)


def per_device(residual, inv_diag, coupling_tiles, colour, tile_cols):
    axis = "rows"
    count = lax.axis_size(axis)
    groups = count // COLOURS
    me = lax.axis_index(axis)
    core = (me % 2).reshape(1)
    place = me % COLOURS
    group = me // COLOURS
    block, cols = residual.shape
    half = cols // 2
    tiles = jnp.transpose(coupling_tiles, (1, 0, 2))
    number = tiles.shape[0]

    def flip(value, bit):
        return lax.ppermute(value, axis, [(i, i ^ bit) for i in range(count)])

    def is_wrap(i, target):
        return abs(i // COLOURS - target // COLOURS) > 1

    def beside(value, ahead, with_wrap):
        pairs = []
        for i in range(count):
            step = COLOURS if (i // 2) % 2 == ahead else -COLOURS
            pairs.append((i, (i + step) % count))
        return lax.ppermute(value, axis, [p for p in pairs if with_wrap or not is_wrap(*p)])

    def around_wrap(value, change):
        pairs = []
        for i in range(count):
            target_chip = (i // 2) % 2 ^ change
            target = (i ^ (2 * change)) + (COLOURS if target_chip == 0 else -COLOURS)
            if not 0 <= target < count:
                pairs.append((i, target % count))
        return lax.ppermute(value, axis, pairs)

    keep, send, own_rows = pl.pallas_call(
        first_kernel,
        out_shape=[pltpu.VMEM((half, block), jnp.float32)]
        + [pltpu.VMEM((half + EXTRA, block), jnp.float32), pltpu.VMEM((EXTRA, block), jnp.float32)],
        in_specs=[smem(), smem(), smem(), hbm(), hbm()],
        out_specs=[vmem()] * 3,
        scratch_shapes=[
            pltpu.VMEM((block, block), jnp.float32),
            pltpu.VMEM((block, cols), jnp.float32),
            pltpu.SemaphoreType.DMA((2,)),
        ],
        compiler_params=params(16),
        name="first",
    )(core, colour, tile_cols, *far([inv_diag, residual]))
    arrived = flip(send, 1)
    starts = [keep, arrived]

    late_tiles, _ = lax.optimization_barrier((tiles, arrived))
    sib_tiles, sib_inverse = flip(late_tiles, 1), flip(inv_diag, 1)

    own_wide, sib_wide = own_rows[:1], arrived[half : half + 1]
    candidate = jnp.where(own_wide == 0, keep, jnp.where(sib_wide == 0, arrived[:half], 0.0))
    wheel = lax.broadcasted_iota(jnp.int32, (EXTRA, block), 0).astype(jnp.float32)
    places = jnp.where(wheel == own_wide, place + 1, 0) + jnp.where(wheel == sib_wide, (place ^ 1) + 1, 0)
    places = places.astype(jnp.float32)
    sent = jnp.concatenate([candidate, places])
    swapped = flip(sent, 2)
    outer = beside(sent, 1, True)
    here = jnp.where((own_wide == 0) | (sib_wide == 0), candidate, swapped[:half])
    here = jnp.concatenate([here, places + swapped[half:]])
    none = jnp.zeros_like(here)
    known = {0: [[beside(here, 0, True), none, none], outer, here]}
    toward = jnp.where(place < COLOURS // 2, -1, 1)
    firsts = jnp.stack([((group + step) % groups) * COLOURS for step in (toward, -toward, 0 * toward)]).astype(jnp.int32)
    far_tiles, far_inverse, _ = lax.optimization_barrier((tiles, inv_diag, here))
    *own_parts, zeros = parts(*far([far_tiles, far_inverse]), [here], "own_parts")
    *sib_parts, zeros = parts(sib_tiles, sib_inverse, [zeros], "sib_parts")
    matrices = [*own_parts, *sib_parts]
    facts = (firsts, own_rows, arrived, known[0])
    order = list(range(1, COLOURS)) + list(range(COLOURS - 2, -1, -1))
    plans, masks = make_plans(number, order[:1], *facts, zeros)
    newest = 0
    sums, used, finals = {}, {}, {}
    partial = []
    for step, now in enumerate(order):
        used[now] = {(c, done_at(order, c, step)) for c in known if c != now}
        outs = relax(now, newest, plans[now], matrices, starts, known[newest], partial, int(now in order[step + 1 :]))
        candidate, sums[now] = outs[0], outs[1:]
        finals[now] = candidate
        if step == len(order) - 1:
            break
        if step == 0:
            rest = [c for c in range(COLOURS) if c not in plans]
            for table, more in zip((plans, masks), make_plans(number, rest, *facts, candidate)):
                table.update(more)
        after = order[step + 1]
        swapped = flip(candidate, 2)
        outer = beside(candidate, 1, True)
        wraps = [around_wrap(candidate, change) for change in range(2)]
        here = jnp.where(masks[now][:1] != 0, candidate, swapped)
        inner = [beside(here, 0, False), *wraps]
        fresh = used.get(after, set())
        older = tuple(c for c in sorted(known) if c not in (now, after) and (c, done_at(order, c, step)) not in fresh)
        partial = [add_older(after, now, older, plans[after], matrices, outer, here, known, sums.get(after, []))]
        known[now] = [inner, outer, here]
        newest = now

    own_final, sib_final = finals[0], finals[0]
    for c in range(1, COLOURS):
        own_final = jnp.where(own_wide == c, finals[c], own_final)
        sib_final = jnp.where(sib_wide == c, finals[c], sib_final)
    mine, other = own_final, flip(sib_final, 1)
    return pl.pallas_call(
        last_kernel,
        out_shape=jax.ShapeDtypeStruct((block, cols), jnp.float32),
        in_specs=[smem(), vmem(), vmem()],
        out_specs=vmem(),
        compiler_params=params(16),
        name="last",
    )(core, *near([mine, other]))


def done_at(order, colour, step):
    return max([i for i in range(step) if order[i] == colour], default=-1)


def solution(mesh):
    in_specs = (P("rows", None), P("rows", None), P("rows", None, None), P("rows"), P("rows", None))
    out_specs = P("rows", None)
    return jax.shard_map(
        per_device, mesh=mesh, in_specs=in_specs, out_specs=out_specs, check_vma=False
    )
```

```python
import functools

import jax
import jax.numpy as jnp
from jax import lax
from jax.experimental import pallas as pl
from jax.experimental.pallas import tpu as pltpu
from jax.sharding import PartitionSpec as P

COLOURS = 4
SIDES = 3
INNER, OUTER, HERE = range(3)
EXTRA = 8
LANES = 128
ACTIVE, IS_OWN, TILE = range(3)


def dot_t(a, b):
    return lax.dot_general(a, b, (((1,), (1,)), ((), ())), preferred_element_type=jnp.float32)


def split(value):
    high = value.astype(jnp.bfloat16)
    return high, (value - high.astype(jnp.float32)).astype(jnp.bfloat16)


def times(value, high, low):
    rows = value.shape[0]
    parts = jnp.concatenate(split(value), axis=0)
    product = dot_t(parts, high) + dot_t(parts, low)
    return product[:rows] + product[rows:]


def vmem():
    return pl.BlockSpec(memory_space=pltpu.VMEM)


def smem():
    return pl.BlockSpec(memory_space=pltpu.SMEM)


def anywhere():
    return pl.BlockSpec(memory_space=pl.ANY)


def hbm():
    return pl.BlockSpec(memory_space=pltpu.HBM)


def params(mebibytes):
    return pltpu.CompilerParams(vmem_limit_bytes=mebibytes * 1024 * 1024)


def far(values):
    return [pltpu.with_memory_space_constraint(v, pltpu.HBM) for v in values]


def near(values):
    return [pltpu.with_memory_space_constraint(v, pltpu.VMEM) for v in values]


def first_kernel(core_ref, colour_ref, tile_cols_ref, inverse_hbm, residual_hbm, keep_ref, send_ref, facts_out, inverse_ref, residual_ref, sems):
    copies = [
        pltpu.make_async_copy(residual_hbm, residual_ref, sems.at[0]),
        pltpu.make_async_copy(inverse_hbm, inverse_ref, sems.at[1]),
    ]
    for copy in copies:
        copy.start()
    for copy in copies:
        copy.wait()
    value = times(jnp.transpose(residual_ref[...]), *split(inverse_ref[...]))
    half, block = keep_ref.shape
    is_first = core_ref[0] == 0
    keep_ref[...] = jnp.where(is_first, value[:half], value[half:])
    send_ref[:half, :] = jnp.where(is_first, value[half:], value[:half])
    row = lax.broadcasted_iota(jnp.int32, (EXTRA, block), 0)
    rows = jnp.where(row == 0, colour_ref[0], 0)
    for k in range(tile_cols_ref.shape[1]):
        rows = jnp.where(row == k + 1, tile_cols_ref[0, k], rows)
    send_ref[half:, :] = rows.astype(jnp.float32)
    facts_out[...] = rows.astype(jnp.float32)


def last_kernel(core_ref, mine_ref, other_ref, out_ref):
    is_first = core_ref[0] == 0
    mine, other = mine_ref[...], other_ref[...]
    first = jnp.where(is_first, mine, other)
    second = jnp.where(is_first, other, mine)
    out_ref[...] = jnp.transpose(jnp.concatenate([first, second], axis=0))


def parts_kernel(tiles_ref, inverse_ref, _, w_high, w_low, zeros, buffer, sems):
    zeros[...] = jnp.zeros_like(zeros)
    tiles = tiles_ref.shape[0]
    copies = [pltpu.make_async_copy(tiles_ref.at[k], buffer.at[k], sems.at[k]) for k in range(tiles)]
    copies.append(pltpu.make_async_copy(inverse_ref, buffer.at[tiles], sems.at[tiles]))
    for copy in copies:
        copy.start()
    for k, copy in enumerate(copies):
        copy.wait()
        w_high[k], w_low[k] = split(buffer[k])


def plan_kernel(tiles, colours, firsts_ref, _, own_rows, arrived, inner, outer, here, *outs):
    half = arrived.shape[0] - EXTRA
    lanes = pl.ds(0, LANES)
    own = own_rows[:, lanes].astype(jnp.int32)
    sib = arrived[half:, lanes].astype(jnp.int32)
    wanted = []
    for side, ref in enumerate((inner, outer, here)):
        found = ref[half:, lanes].astype(jnp.int32)
        wanted.append(jnp.where(found > 0, firsts_ref[side] + found - 1, -1))
    rows = outs[0].shape[0]
    row = lax.broadcasted_iota(jnp.int32, (rows, LANES), 0)
    for i, now in enumerate(colours):
        is_own, is_sib = own[:1] == now, sib[:1] == now
        active = (is_own | is_sib).astype(jnp.int32)
        plan = jnp.where(row == ACTIVE, active, is_own.astype(jnp.int32))
        listed = [jnp.where(is_own, own[k + 1 : k + 2], sib[k + 1 : k + 2]) for k in range(tiles)]
        for side in range(SIDES):
            found = jnp.full((EXTRA, LANES), -1, jnp.int32)
            for k in range(tiles):
                found = jnp.where(wanted[side] == listed[k], k, found)
            for c in range(COLOURS):
                plan = jnp.where(row == TILE + side * COLOURS + c, found[c : c + 1], plan)
        outs[i][...] = plan
        mask = outs[len(colours) + i]
        mask[...] = jnp.concatenate([jnp.broadcast_to(active, (EXTRA, LANES))] * (mask.shape[1] // LANES), axis=1)


def chosen(plan, body, own, sib):
    active, is_own = plan[ACTIVE, 0] != 0, plan[IS_OWN, 0] != 0

    @pl.when(active & is_own)
    def _():
        body(*own)

    @pl.when(active & jnp.logical_not(is_own))
    def _():
        body(*sib)


def older_kernel(newest, older, has_base, plan, own_high, own_low, sib_high, sib_low, outer, here, *refs):
    *refs, partial = refs
    known, base = refs[: SIDES * len(older)], refs[SIDES * len(older) :]
    half = partial.shape[0]
    slots = [(newest, OUTER, outer), (newest, HERE, here)]
    slots += [(c, side, known[SIDES * i + side]) for i, c in enumerate(older) for side in range(SIDES)]

    def body(w_high, w_low):
        partial[...] = base[0][...] if has_base else jnp.zeros_like(partial)
        for c, side, ref in slots:
            k = plan[TILE + side * COLOURS + c, 0]

            @pl.when(k >= 0)
            def _():
                partial[...] += times(ref[:half, :], w_high[k], w_low[k])

    chosen(plan, body, (own_high, own_low), (sib_high, sib_low))


def relax_kernel(newest, sides, plan, own_high, own_low, sib_high, sib_low, own_start, sib_start, *refs):
    latest, refs = refs[:sides], refs[sides:]
    base, refs = refs[: int(sides < SIDES)], refs[int(sides < SIDES) :]
    out, total = refs[:2]
    half = out.shape[0]

    def body(w_high, w_low, begin):
        total[...] = base[0][...] if base else jnp.zeros_like(total)
        for side, ref in enumerate(latest):
            k = plan[TILE + side * COLOURS + newest, 0]

            @pl.when(k >= 0)
            def _():
                total[...] += times(ref[:half, :], w_high[k], w_low[k])

        last = w_high.shape[0] - 1
        out[...] = begin[:half, :] - times(total[...], w_high[last], w_low[last])

    chosen(plan, body, (own_high, own_low, own_start), (sib_high, sib_low, sib_start))

    @pl.when(plan[ACTIVE, 0] == 0)
    def _():
        out[...] = jnp.zeros_like(out)


def parts(tiles, inverse, after, name):
    count, block, _ = tiles.shape
    shape = (count + 1, block, block)
    return pl.pallas_call(
        parts_kernel,
        out_shape=[pltpu.VMEM(shape, jnp.bfloat16)] * 2 + [pltpu.VMEM((EXTRA, block), jnp.float32)],
        in_specs=[anywhere()] * 3,
        out_specs=[vmem()] * 3,
        scratch_shapes=[pltpu.VMEM(shape, jnp.float32), pltpu.SemaphoreType.DMA((count + 1,))],
        compiler_params=params(12),
        cost_estimate=pl.CostEstimate(flops=0, bytes_accessed=8 * count * block * block, transcendentals=0),
        name=name,
    )(tiles, inverse, *after)


def make_plans(tiles, colours, firsts, own_rows, arrived, first_known, zeros):
    block = own_rows.shape[1]
    rows = -(-(TILE + SIDES * COLOURS) // EXTRA) * EXTRA
    number = len(colours)
    outs = pl.pallas_call(
        functools.partial(plan_kernel, tiles, colours),
        out_shape=[pltpu.VMEM((rows, LANES), jnp.int32)] * number + [pltpu.VMEM((EXTRA, block), jnp.int32)] * number,
        in_specs=[smem()] + [vmem()] * 6,
        out_specs=[vmem()] * (2 * number),
        compiler_params=params(8),
        name=f"plan_{number}",
    )(firsts, *near([zeros, own_rows, arrived, *first_known]))
    return dict(zip(colours, outs[:number])), dict(zip(colours, outs[number:]))


def add_older(now, newest, older, plan, matrices, outer, here, known, base):
    half, block = here.shape
    operands = near([plan, *matrices, outer, here, *[value for c in older for value in known[c]], *base])
    slots = 2 + SIDES * len(older)
    return pl.pallas_call(
        functools.partial(older_kernel, newest, older, len(base)),
        out_shape=pltpu.VMEM((half, block), jnp.float32),
        in_specs=[vmem()] * len(operands),
        out_specs=vmem(),
        compiler_params=params(8),
        cost_estimate=pl.CostEstimate(
            flops=4 * block * block * LANES * slots, bytes_accessed=4 * block * block * slots, transcendentals=0
        ),
        name=f"older_{now}",
    )(*operands)


def relax(now, newest, plan, matrices, starts, latest, partial, keep_sum):
    half, block = starts[0].shape
    sides = 1 if partial else SIDES
    operands = near([plan, *matrices, *starts, *latest[:sides], *partial])
    value = pltpu.VMEM((half, block), jnp.float32)
    return pl.pallas_call(
        functools.partial(relax_kernel, newest, sides),
        out_shape=[value] * (1 + keep_sum),
        in_specs=[vmem()] * len(operands),
        out_specs=[vmem()] * (1 + keep_sum),
        scratch_shapes=[value] * (1 - keep_sum),
        compiler_params=params(8),
        cost_estimate=pl.CostEstimate(
            flops=16 * block * block * LANES, bytes_accessed=16 * block * block, transcendentals=0
        ),
        name=f"relax_{now}",
    )(*operands)


def per_device(residual, inv_diag, coupling_tiles, colour, tile_cols):
    axis = "rows"
    count = lax.axis_size(axis)
    groups = count // COLOURS
    me = lax.axis_index(axis)
    core = (me % 2).reshape(1)
    place = me % COLOURS
    group = me // COLOURS
    block, cols = residual.shape
    half = cols // 2
    tiles = jnp.transpose(coupling_tiles, (1, 0, 2))
    number = tiles.shape[0]

    def flip(value, bit):
        return lax.ppermute(value, axis, [(i, i ^ bit) for i in range(count)])

    def beside(value, ahead):
        pairs = []
        for i in range(count):
            step = COLOURS if (i // 2) % 2 == ahead else -COLOURS
            pairs.append((i, (i + step) % count))
        return lax.ppermute(value, axis, pairs)

    keep, send, own_rows = pl.pallas_call(
        first_kernel,
        out_shape=[pltpu.VMEM((half, block), jnp.float32)]
        + [pltpu.VMEM((half + EXTRA, block), jnp.float32), pltpu.VMEM((EXTRA, block), jnp.float32)],
        in_specs=[smem(), smem(), smem(), hbm(), hbm()],
        out_specs=[vmem()] * 3,
        scratch_shapes=[
            pltpu.VMEM((block, block), jnp.float32),
            pltpu.VMEM((block, cols), jnp.float32),
            pltpu.SemaphoreType.DMA((2,)),
        ],
        compiler_params=params(16),
        name="first",
    )(core, colour, tile_cols, *far([inv_diag, residual]))
    arrived = flip(send, 1)
    starts = [keep, arrived]

    late_tiles, _ = lax.optimization_barrier((tiles, arrived))
    sib_tiles, sib_inverse = flip(late_tiles, 1), flip(inv_diag, 1)

    own_wide, sib_wide = own_rows[:1], arrived[half : half + 1]
    candidate = jnp.where(own_wide == 0, keep, jnp.where(sib_wide == 0, arrived[:half], 0.0))
    wheel = lax.broadcasted_iota(jnp.int32, (EXTRA, block), 0).astype(jnp.float32)
    places = jnp.where(wheel == own_wide, place + 1, 0) + jnp.where(wheel == sib_wide, (place ^ 1) + 1, 0)
    places = places.astype(jnp.float32)
    sent = jnp.concatenate([candidate, places])
    swapped = flip(sent, 2)
    outer = beside(sent, 1)
    here = jnp.where((own_wide == 0) | (sib_wide == 0), candidate, swapped[:half])
    here = jnp.concatenate([here, places + swapped[half:]])
    known = {0: [beside(here, 0), outer, here]}
    toward = jnp.where(place < COLOURS // 2, -1, 1)
    firsts = jnp.stack([((group + step) % groups) * COLOURS for step in (toward, -toward, 0 * toward)]).astype(jnp.int32)
    far_tiles, far_inverse, _ = lax.optimization_barrier((tiles, inv_diag, here))
    *own_parts, zeros = parts(*far([far_tiles, far_inverse]), [here], "own_parts")
    *sib_parts, zeros = parts(sib_tiles, sib_inverse, [zeros], "sib_parts")
    matrices = [*own_parts, *sib_parts]
    facts = (firsts, own_rows, arrived, known[0])
    order = list(range(1, COLOURS)) + list(range(COLOURS - 2, -1, -1))
    plans, masks = make_plans(number, order[:1], *facts, zeros)
    newest = 0
    sums, used, finals = {}, {}, {}
    partial = []
    for step, now in enumerate(order):
        used[now] = {(c, done_at(order, c, step)) for c in known if c != now}
        outs = relax(now, newest, plans[now], matrices, starts, known[newest], partial, int(now in order[step + 1 :]))
        candidate, sums[now] = outs[0], outs[1:]
        finals[now] = candidate
        if step == len(order) - 1:
            break
        if step == 0:
            rest = [c for c in range(COLOURS) if c not in plans]
            for table, more in zip((plans, masks), make_plans(number, rest, *facts, candidate)):
                table.update(more)
        after = order[step + 1]
        swapped = flip(candidate, 2)
        outer = beside(candidate, 1)
        here = jnp.where(masks[now][:1] != 0, candidate, swapped)
        inner = beside(here, 0)
        fresh = used.get(after, set())
        older = tuple(c for c in sorted(known) if c not in (now, after) and (c, done_at(order, c, step)) not in fresh)
        partial = [add_older(after, now, older, plans[after], matrices, outer, here, known, sums.get(after, []))]
        known[now] = [inner, outer, here]
        newest = now

    own_final, sib_final = finals[0], finals[0]
    for c in range(1, COLOURS):
        own_final = jnp.where(own_wide == c, finals[c], own_final)
        sib_final = jnp.where(sib_wide == c, finals[c], sib_final)
    mine, other = own_final, flip(sib_final, 1)
    return pl.pallas_call(
        last_kernel,
        out_shape=jax.ShapeDtypeStruct((block, cols), jnp.float32),
        in_specs=[smem(), vmem(), vmem()],
        out_specs=vmem(),
        compiler_params=params(16),
        name="last",
    )(core, *near([mine, other]))


def done_at(order, colour, step):
    return max([i for i in range(step) if order[i] == colour], default=-1)


def solution(mesh):
    in_specs = (P("rows", None), P("rows", None), P("rows", None, None), P("rows"), P("rows", None))
    out_specs = P("rows", None)
    return jax.shard_map(
        per_device, mesh=mesh, in_specs=in_specs, out_specs=out_specs, check_vma=False
    )
```

```python
import functools

import jax
import jax.numpy as jnp
from jax import lax
from jax.experimental import pallas as pl
from jax.experimental.pallas import tpu as pltpu
from jax.sharding import PartitionSpec as P

COLOURS = 4
SIDES = 3
INNER, OUTER, HERE = range(3)
EXTRA = 8
LANES = 128
ACTIVE, IS_OWN, TILE = range(3)


def dot_t(a, b):
    return lax.dot_general(a, b, (((1,), (1,)), ((), ())), preferred_element_type=jnp.float32)


def dot(a, b):
    return jnp.dot(a, b, preferred_element_type=jnp.float32)


def split(value):
    high = value.astype(jnp.bfloat16)
    return high, (value - high.astype(jnp.float32)).astype(jnp.bfloat16)


def times(value, high, low):
    rows = value.shape[0]
    parts = jnp.concatenate(split(value), axis=0)
    product = dot_t(parts, high) + dot_t(parts, low)
    return product[:rows] + product[rows:]


def vmem():
    return pl.BlockSpec(memory_space=pltpu.VMEM)


def smem():
    return pl.BlockSpec(memory_space=pltpu.SMEM)


def anywhere():
    return pl.BlockSpec(memory_space=pl.ANY)


def hbm():
    return pl.BlockSpec(memory_space=pltpu.HBM)


def params(mebibytes):
    return pltpu.CompilerParams(vmem_limit_bytes=mebibytes * 1024 * 1024)


def far(values):
    return [pltpu.with_memory_space_constraint(v, pltpu.HBM) for v in values]


def near(values):
    return [pltpu.with_memory_space_constraint(v, pltpu.VMEM) for v in values]


def first_kernel(core_ref, colour_ref, tile_cols_ref, inverse_hbm, residual_hbm, keep_ref, send_ref, facts_out, inverse_ref, residual_ref, sems):
    copies = [
        pltpu.make_async_copy(residual_hbm, residual_ref, sems.at[0]),
        pltpu.make_async_copy(inverse_hbm, inverse_ref, sems.at[1]),
    ]
    for copy in copies:
        copy.start()
    for copy in copies:
        copy.wait()
    value = times(jnp.transpose(residual_ref[...]), *split(inverse_ref[...]))
    half, block = keep_ref.shape
    is_first = core_ref[0] == 0
    keep_ref[...] = jnp.where(is_first, value[:half], value[half:])
    send_ref[:half, :] = jnp.where(is_first, value[half:], value[:half])
    row = lax.broadcasted_iota(jnp.int32, (EXTRA, block), 0)
    rows = jnp.where(row == 0, colour_ref[0], 0)
    for k in range(tile_cols_ref.shape[1]):
        rows = jnp.where(row == k + 1, tile_cols_ref[0, k], rows)
    send_ref[half:, :] = rows.astype(jnp.float32)
    facts_out[...] = rows.astype(jnp.float32)


def last_kernel(core_ref, mine_ref, other_ref, out_ref):
    is_first = core_ref[0] == 0
    mine, other = mine_ref[...], other_ref[...]
    first = jnp.where(is_first, mine, other)
    second = jnp.where(is_first, other, mine)
    out_ref[...] = jnp.transpose(jnp.concatenate([first, second], axis=0))


def parts_kernel(tiles_ref, inverse_ref, _, w_high, w_low, zeros, buffer, sems):
    zeros[...] = jnp.zeros_like(zeros)
    tiles = tiles_ref.shape[0]
    copies = [pltpu.make_async_copy(tiles_ref.at[k], buffer.at[k], sems.at[k]) for k in range(tiles)]
    copies.append(pltpu.make_async_copy(inverse_ref, buffer.at[tiles], sems.at[tiles]))
    for copy in copies:
        copy.start()
    for k, copy in enumerate(copies):
        copy.wait()
        w_high[k], w_low[k] = split(buffer[k])


def plan_kernel(tiles, colours, firsts_ref, _, own_rows, arrived, inner, outer, here, *outs):
    half = arrived.shape[0] - EXTRA
    lanes = pl.ds(0, LANES)
    own = own_rows[:, lanes].astype(jnp.int32)
    sib = arrived[half:, lanes].astype(jnp.int32)
    wanted = []
    for side, ref in enumerate((inner, outer, here)):
        found = ref[half:, lanes].astype(jnp.int32)
        wanted.append(jnp.where(found > 0, firsts_ref[side] + found - 1, -1))
    rows = outs[0].shape[0]
    row = lax.broadcasted_iota(jnp.int32, (rows, LANES), 0)
    for i, now in enumerate(colours):
        is_own, is_sib = own[:1] == now, sib[:1] == now
        active = (is_own | is_sib).astype(jnp.int32)
        plan = jnp.where(row == ACTIVE, active, is_own.astype(jnp.int32))
        listed = [jnp.where(is_own, own[k + 1 : k + 2], sib[k + 1 : k + 2]) for k in range(tiles)]
        for side in range(SIDES):
            found = jnp.full((EXTRA, LANES), -1, jnp.int32)
            for k in range(tiles):
                found = jnp.where(wanted[side] == listed[k], k, found)
            for c in range(COLOURS):
                plan = jnp.where(row == TILE + side * COLOURS + c, found[c : c + 1], plan)
        outs[i][...] = plan
        mask = outs[len(colours) + i]
        mask[...] = jnp.concatenate([jnp.broadcast_to(active, (EXTRA, LANES))] * (mask.shape[1] // LANES), axis=1)


def chosen(plan, body, own, sib):
    active, is_own = plan[ACTIVE, 0] != 0, plan[IS_OWN, 0] != 0

    @pl.when(active & is_own)
    def _():
        body(*own)

    @pl.when(active & jnp.logical_not(is_own))
    def _():
        body(*sib)


def older_kernel(newest, slots, has_base, plan, own_high, own_low, sib_high, sib_low, own_start, sib_start, outer, here, *refs):
    *refs, partial, begin, m_high, m_low = refs
    known, base = refs[: len(slots)], refs[len(slots) :]
    half = partial.shape[0]
    slots = [(newest, OUTER, outer), (newest, HERE, here)] + [(*slot, ref) for slot, ref in zip(slots, known)]

    def body(w_high, w_low, start):
        last = w_high.shape[0] - 1
        inner = plan[TILE + INNER * COLOURS + newest, 0]

        @pl.when(inner >= 0)
        def _():
            high, low = w_high[last], w_low[last]
            tile_high, tile_low = w_high[inner], w_low[inner]
            m_high[...], m_low[...] = split(dot(high, tile_high) + (dot(high, tile_low) + dot(low, tile_high)))

        partial[...] = base[0][...] if has_base else jnp.zeros_like(partial)
        for c, side, ref in slots:
            k = plan[TILE + side * COLOURS + c, 0]

            @pl.when(k >= 0)
            def _():
                partial[...] += times(ref[:half, :], w_high[k], w_low[k])

        begin[...] = start[:half, :] - times(partial[...], w_high[last], w_low[last])

    chosen(plan, body, (own_high, own_low, own_start), (sib_high, sib_low, sib_start))


def relax_kernel(newest, plan, inner, begin, m_high, m_low, out):
    active = plan[ACTIVE, 0] != 0
    meets = plan[TILE + INNER * COLOURS + newest, 0] >= 0

    @pl.when(active & meets)
    def _():
        out[...] = begin[...] - times(inner[...], m_high[...], m_low[...])

    @pl.when(active & jnp.logical_not(meets))
    def _():
        out[...] = begin[...]

    @pl.when(jnp.logical_not(active))
    def _():
        out[...] = jnp.zeros_like(out)


def first_relax_kernel(newest, plan, own_high, own_low, sib_high, sib_low, own_start, sib_start, *refs):
    *latest, out, total = refs
    half = out.shape[0]

    def body(w_high, w_low, begin):
        total[...] = jnp.zeros_like(total)
        for side, ref in enumerate(latest):
            k = plan[TILE + side * COLOURS + newest, 0]

            @pl.when(k >= 0)
            def _():
                total[...] += times(ref[:half, :], w_high[k], w_low[k])

        last = w_high.shape[0] - 1
        out[...] = begin[:half, :] - times(total[...], w_high[last], w_low[last])

    chosen(plan, body, (own_high, own_low, own_start), (sib_high, sib_low, sib_start))

    @pl.when(plan[ACTIVE, 0] == 0)
    def _():
        out[...] = jnp.zeros_like(out)


def parts(tiles, inverse, after, name):
    count, block, _ = tiles.shape
    shape = (count + 1, block, block)
    return pl.pallas_call(
        parts_kernel,
        out_shape=[pltpu.VMEM(shape, jnp.bfloat16)] * 2 + [pltpu.VMEM((EXTRA, block), jnp.float32)],
        in_specs=[anywhere()] * 3,
        out_specs=[vmem()] * 3,
        scratch_shapes=[pltpu.VMEM(shape, jnp.float32), pltpu.SemaphoreType.DMA((count + 1,))],
        compiler_params=params(12),
        cost_estimate=pl.CostEstimate(flops=0, bytes_accessed=8 * count * block * block, transcendentals=0),
        name=name,
    )(tiles, inverse, *after)


def make_plans(tiles, colours, firsts, own_rows, arrived, first_known, zeros):
    block = own_rows.shape[1]
    rows = -(-(TILE + SIDES * COLOURS) // EXTRA) * EXTRA
    number = len(colours)
    outs = pl.pallas_call(
        functools.partial(plan_kernel, tiles, colours),
        out_shape=[pltpu.VMEM((rows, LANES), jnp.int32)] * number + [pltpu.VMEM((EXTRA, block), jnp.int32)] * number,
        in_specs=[smem()] + [vmem()] * 6,
        out_specs=[vmem()] * (2 * number),
        compiler_params=params(8),
        name=f"plan_{number}",
    )(firsts, *near([zeros, own_rows, arrived, *first_known]))
    return dict(zip(colours, outs[:number])), dict(zip(colours, outs[number:]))


def add_older(now, newest, slots, plan, matrices, starts, outer, here, known, base):
    half, block = starts[0].shape
    operands = near([plan, *matrices, *starts, outer, here, *[known[c][side] for c, side in slots], *base])
    value, matrix = pltpu.VMEM((half, block), jnp.float32), pltpu.VMEM((block, block), jnp.bfloat16)
    return pl.pallas_call(
        functools.partial(older_kernel, newest, slots, len(base)),
        out_shape=[value, value, matrix, matrix],
        in_specs=[vmem()] * len(operands),
        out_specs=[vmem()] * 4,
        compiler_params=params(16),
        cost_estimate=pl.CostEstimate(
            flops=4 * block * block * LANES * (2 + len(slots)), bytes_accessed=24 * block * block, transcendentals=0
        ),
        name=f"older_{now}",
    )(*operands)


def run_relax(name, kernel, operands, half, block, outs):
    return pl.pallas_call(
        kernel,
        out_shape=[pltpu.VMEM((half, block), jnp.float32)] * outs,
        in_specs=[vmem()] * len(operands),
        out_specs=[vmem()] * outs,
        compiler_params=params(8),
        cost_estimate=pl.CostEstimate(
            flops=16 * block * block * LANES, bytes_accessed=16 * block * block, transcendentals=0
        ),
        name=name,
    )(*near(operands))


def per_device(residual, inv_diag, coupling_tiles, colour, tile_cols):
    axis = "rows"
    count = lax.axis_size(axis)
    groups = count // COLOURS
    me = lax.axis_index(axis)
    core = (me % 2).reshape(1)
    place = me % COLOURS
    group = me // COLOURS
    block, cols = residual.shape
    half = cols // 2
    tiles = jnp.transpose(coupling_tiles, (1, 0, 2))
    number = tiles.shape[0]

    def flip(value, bit):
        return lax.ppermute(value, axis, [(i, i ^ bit) for i in range(count)])

    def beside(value, ahead):
        pairs = []
        for i in range(count):
            step = COLOURS if (i // 2) % 2 == ahead else -COLOURS
            pairs.append((i, (i + step) % count))
        return lax.ppermute(value, axis, pairs)

    keep, send, own_rows = pl.pallas_call(
        first_kernel,
        out_shape=[pltpu.VMEM((half, block), jnp.float32)]
        + [pltpu.VMEM((half + EXTRA, block), jnp.float32), pltpu.VMEM((EXTRA, block), jnp.float32)],
        in_specs=[smem(), smem(), smem(), hbm(), hbm()],
        out_specs=[vmem()] * 3,
        scratch_shapes=[
            pltpu.VMEM((block, block), jnp.float32),
            pltpu.VMEM((block, cols), jnp.float32),
            pltpu.SemaphoreType.DMA((2,)),
        ],
        compiler_params=params(16),
        name="first",
    )(core, colour, tile_cols, *far([inv_diag, residual]))
    arrived = flip(send, 1)
    starts = [keep, arrived]

    late_tiles, _ = lax.optimization_barrier((tiles, arrived))
    sib_tiles, sib_inverse = flip(late_tiles, 1), flip(inv_diag, 1)

    own_wide, sib_wide = own_rows[:1], arrived[half : half + 1]
    candidate = jnp.where(own_wide == 0, keep, jnp.where(sib_wide == 0, arrived[:half], 0.0))
    wheel = lax.broadcasted_iota(jnp.int32, (EXTRA, block), 0).astype(jnp.float32)
    places = jnp.where(wheel == own_wide, place + 1, 0) + jnp.where(wheel == sib_wide, (place ^ 1) + 1, 0)
    places = places.astype(jnp.float32)
    sent = jnp.concatenate([candidate, places])
    swapped = flip(sent, 2)
    outer = beside(sent, 1)
    here = jnp.where((own_wide == 0) | (sib_wide == 0), candidate, swapped[:half])
    here = jnp.concatenate([here, places + swapped[half:]])
    known = {0: [beside(here, 0), outer, here]}
    toward = jnp.where(place < COLOURS // 2, -1, 1)
    firsts = jnp.stack([((group + step) % groups) * COLOURS for step in (toward, -toward, 0 * toward)]).astype(jnp.int32)
    far_tiles, far_inverse, _ = lax.optimization_barrier((tiles, inv_diag, here))
    *own_parts, zeros = parts(*far([far_tiles, far_inverse]), [here], "own_parts")
    *sib_parts, zeros = parts(sib_tiles, sib_inverse, [zeros], "sib_parts")
    matrices = [*own_parts, *sib_parts]
    facts = (firsts, own_rows, arrived, known[0])
    order = list(range(1, COLOURS)) + list(range(COLOURS - 2, -1, -1))
    plans, masks = make_plans(number, order[:1], *facts, zeros)
    newest = 0
    bases, included, finals = {}, {}, {}
    for step, now in enumerate(order):
        if step == 0:
            operands = [plans[now], *matrices, *starts, *known[newest]]
            kernel = functools.partial(first_relax_kernel, newest)
            candidate, bases[now] = run_relax(f"relax_{now}", kernel, operands, half, block, 2)
            included[now] = {(newest, -1, side) for side in range(SIDES)}
        else:
            operands = [plans[now], known[newest][INNER], *update]
            kernel = functools.partial(relax_kernel, newest)
            (candidate,) = run_relax(f"relax_{now}", kernel, operands, half, block, 1)
        finals[now] = candidate
        if step == len(order) - 1:
            break
        if step == 0:
            rest = [c for c in range(COLOURS) if c not in plans]
            for table, more in zip((plans, masks), make_plans(number, rest, *facts, candidate)):
                table.update(more)
        after = order[step + 1]
        swapped = flip(candidate, 2)
        outer = beside(candidate, 1)
        here = jnp.where(masks[now][:1] != 0, candidate, swapped)
        inner = beside(here, 0)
        have = included.get(after, set())
        slots, all_slots = [], {(now, step, OUTER), (now, step, HERE)}
        for c in sorted(known):
            for side in range(SIDES):
                if c not in (now, after):
                    all_slots.add((c, done_at(order, c, step), side))
                    if (c, done_at(order, c, step), side) not in have:
                        slots.append((c, side))
        base = [bases[after]] if after in bases else []
        partial, *update = add_older(after, now, slots, plans[after], matrices, starts, outer, here, known, base)
        bases[after], included[after] = partial, all_slots
        known[now] = [inner, outer, here]
        newest = now

    own_final, sib_final = finals[0], finals[0]
    for c in range(1, COLOURS):
        own_final = jnp.where(own_wide == c, finals[c], own_final)
        sib_final = jnp.where(sib_wide == c, finals[c], sib_final)
    mine, other = own_final, flip(sib_final, 1)
    return pl.pallas_call(
        last_kernel,
        out_shape=jax.ShapeDtypeStruct((block, cols), jnp.float32),
        in_specs=[smem(), vmem(), vmem()],
        out_specs=vmem(),
        compiler_params=params(16),
        name="last",
    )(core, *near([mine, other]))


def done_at(order, colour, step):
    return max([i for i in range(step) if order[i] == colour], default=-1)


def solution(mesh):
    in_specs = (P("rows", None), P("rows", None), P("rows", None, None), P("rows"), P("rows", None))
    out_specs = P("rows", None)
    return jax.shard_map(
        per_device, mesh=mesh, in_specs=in_specs, out_specs=out_specs, check_vma=False
    )
```

```python
import functools

import jax
import jax.numpy as jnp
from jax import lax
from jax.experimental import pallas as pl
from jax.experimental.pallas import tpu as pltpu
from jax.sharding import PartitionSpec as P

COLOURS = 4
SIDES = 3
INNER, OUTER, HERE = range(3)
EXTRA = 8
LANES = 128
ACTIVE, IS_OWN, TILE = range(3)


def dot_t(a, b):
    return lax.dot_general(a, b, (((1,), (1,)), ((), ())), preferred_element_type=jnp.float32)


def dot(a, b):
    return jnp.dot(a, b, preferred_element_type=jnp.float32)


def split(value):
    high = value.astype(jnp.bfloat16)
    return high, (value - high.astype(jnp.float32)).astype(jnp.bfloat16)


def times(value, high, low):
    rows = value.shape[0]
    parts = jnp.concatenate(split(value), axis=0)
    product = dot_t(parts, high) + dot_t(parts, low)
    return product[:rows] + product[rows:]


def vmem():
    return pl.BlockSpec(memory_space=pltpu.VMEM)


def smem():
    return pl.BlockSpec(memory_space=pltpu.SMEM)


def anywhere():
    return pl.BlockSpec(memory_space=pl.ANY)


def hbm():
    return pl.BlockSpec(memory_space=pltpu.HBM)


def params(mebibytes):
    return pltpu.CompilerParams(vmem_limit_bytes=mebibytes * 1024 * 1024)


def far(values):
    return [pltpu.with_memory_space_constraint(v, pltpu.HBM) for v in values]


def near(values):
    return [pltpu.with_memory_space_constraint(v, pltpu.VMEM) for v in values]


def first_kernel(core_ref, colour_ref, tile_cols_ref, inverse_hbm, residual_hbm, keep_ref, send_ref, facts_out, inverse_ref, residual_ref, sems):
    copies = [
        pltpu.make_async_copy(residual_hbm, residual_ref, sems.at[0]),
        pltpu.make_async_copy(inverse_hbm, inverse_ref, sems.at[1]),
    ]
    for copy in copies:
        copy.start()
    for copy in copies:
        copy.wait()
    value = times(jnp.transpose(residual_ref[...]), *split(inverse_ref[...]))
    half, block = keep_ref.shape
    is_first = core_ref[0] == 0
    keep_ref[...] = jnp.where(is_first, value[:half], value[half:])
    send_ref[:half, :] = jnp.where(is_first, value[half:], value[:half])
    row = lax.broadcasted_iota(jnp.int32, (EXTRA, block), 0)
    rows = jnp.where(row == 0, colour_ref[0], 0)
    for k in range(tile_cols_ref.shape[1]):
        rows = jnp.where(row == k + 1, tile_cols_ref[0, k], rows)
    send_ref[half:, :] = rows.astype(jnp.float32)
    facts_out[...] = rows.astype(jnp.float32)


def last_kernel(core_ref, mine_ref, other_ref, out_ref):
    is_first = core_ref[0] == 0
    mine, other = mine_ref[...], other_ref[...]
    first = jnp.where(is_first, mine, other)
    second = jnp.where(is_first, other, mine)
    out_ref[...] = jnp.transpose(jnp.concatenate([first, second], axis=0))


def parts_kernel(tiles_ref, inverse_ref, _, w_high, w_low, zeros, buffer, sems):
    zeros[...] = jnp.zeros_like(zeros)
    tiles = tiles_ref.shape[0]
    copies = [pltpu.make_async_copy(tiles_ref.at[k], buffer.at[k], sems.at[k]) for k in range(tiles)]
    copies.append(pltpu.make_async_copy(inverse_ref, buffer.at[tiles], sems.at[tiles]))
    for copy in copies:
        copy.start()
    for k, copy in enumerate(copies):
        copy.wait()
        w_high[k], w_low[k] = split(buffer[k])


def plan_kernel(tiles, colours, firsts_ref, _, own_rows, arrived, inner, outer, here, *outs):
    half = arrived.shape[0] - EXTRA
    lanes = pl.ds(0, LANES)
    own = own_rows[:, lanes].astype(jnp.int32)
    sib = arrived[half:, lanes].astype(jnp.int32)
    wanted = []
    for side, ref in enumerate((inner, outer, here)):
        found = ref[half:, lanes].astype(jnp.int32)
        wanted.append(jnp.where(found > 0, firsts_ref[side] + found - 1, -1))
    rows = outs[0].shape[0]
    row = lax.broadcasted_iota(jnp.int32, (rows, LANES), 0)
    for i, now in enumerate(colours):
        is_own, is_sib = own[:1] == now, sib[:1] == now
        active = (is_own | is_sib).astype(jnp.int32)
        plan = jnp.where(row == ACTIVE, active, is_own.astype(jnp.int32))
        listed = [jnp.where(is_own, own[k + 1 : k + 2], sib[k + 1 : k + 2]) for k in range(tiles)]
        for side in range(SIDES):
            found = jnp.full((EXTRA, LANES), -1, jnp.int32)
            for k in range(tiles):
                found = jnp.where(wanted[side] == listed[k], k, found)
            for c in range(COLOURS):
                plan = jnp.where(row == TILE + side * COLOURS + c, found[c : c + 1], plan)
        outs[i][...] = plan
        mask = outs[len(colours) + i]
        mask[...] = jnp.concatenate([jnp.broadcast_to(active, (EXTRA, LANES))] * (mask.shape[1] // LANES), axis=1)


def chosen(plan, body, own, sib):
    active, is_own = plan[ACTIVE, 0] != 0, plan[IS_OWN, 0] != 0

    @pl.when(active & is_own)
    def _():
        body(*own)

    @pl.when(active & jnp.logical_not(is_own))
    def _():
        body(*sib)


def older_kernel(newest, slots, has_base, plan, own_high, own_low, sib_high, sib_low, own_start, sib_start, outer, here, *refs):
    *refs, partial, begin, m_high, m_low = refs
    known, base = refs[: len(slots)], refs[len(slots) :]
    half = partial.shape[0]
    slots = [(newest, OUTER, outer), (newest, HERE, here)] + [(*slot, ref) for slot, ref in zip(slots, known)]

    def body(w_high, w_low, start):
        last = w_high.shape[0] - 1
        inner = plan[TILE + INNER * COLOURS + newest, 0]

        @pl.when(inner >= 0)
        def _():
            high, low = w_high[last], w_low[last]
            tile_high, tile_low = w_high[inner], w_low[inner]
            m_high[...], m_low[...] = split(dot(high, tile_high) + (dot(high, tile_low) + dot(low, tile_high)))

        partial[...] = base[0][...] if has_base else jnp.zeros_like(partial)
        for c, side, ref in slots:
            k = plan[TILE + side * COLOURS + c, 0]

            @pl.when(k >= 0)
            def _():
                partial[...] += times(ref[:half, :], w_high[k], w_low[k])

        begin[...] = start[:half, :] - times(partial[...], w_high[last], w_low[last])

    chosen(plan, body, (own_high, own_low, own_start), (sib_high, sib_low, sib_start))


def relax_kernel(newest, plan, inner, begin, m_high, m_low, out):
    active = plan[ACTIVE, 0] != 0
    meets = plan[TILE + INNER * COLOURS + newest, 0] >= 0

    @pl.when(active & meets)
    def _():
        out[...] = begin[...] - times(inner[...], m_high[...], m_low[...])

    @pl.when(active & jnp.logical_not(meets))
    def _():
        out[...] = begin[...]

    @pl.when(jnp.logical_not(active))
    def _():
        out[...] = jnp.zeros_like(out)


def first_relax_kernel(newest, plan, own_high, own_low, sib_high, sib_low, own_start, sib_start, *refs):
    *latest, out, total = refs
    half = out.shape[0]

    def body(w_high, w_low, begin):
        total[...] = jnp.zeros_like(total)
        for side, ref in enumerate(latest):
            k = plan[TILE + side * COLOURS + newest, 0]

            @pl.when(k >= 0)
            def _():
                total[...] += times(ref[:half, :], w_high[k], w_low[k])

        last = w_high.shape[0] - 1
        out[...] = begin[:half, :] - times(total[...], w_high[last], w_low[last])

    chosen(plan, body, (own_high, own_low, own_start), (sib_high, sib_low, sib_start))

    @pl.when(plan[ACTIVE, 0] == 0)
    def _():
        out[...] = jnp.zeros_like(out)


def parts(tiles, inverse, after, name):
    count, block, _ = tiles.shape
    shape = (count + 1, block, block)
    return pl.pallas_call(
        parts_kernel,
        out_shape=[pltpu.VMEM(shape, jnp.bfloat16)] * 2 + [pltpu.VMEM((EXTRA, block), jnp.float32)],
        in_specs=[anywhere()] * 3,
        out_specs=[vmem()] * 3,
        scratch_shapes=[pltpu.VMEM(shape, jnp.float32), pltpu.SemaphoreType.DMA((count + 1,))],
        compiler_params=params(12),
        cost_estimate=pl.CostEstimate(flops=0, bytes_accessed=8 * count * block * block, transcendentals=0),
        name=name,
    )(tiles, inverse, *after)


def make_plans(tiles, colours, firsts, own_rows, arrived, first_known, zeros):
    block = own_rows.shape[1]
    rows = -(-(TILE + SIDES * COLOURS) // EXTRA) * EXTRA
    number = len(colours)
    outs = pl.pallas_call(
        functools.partial(plan_kernel, tiles, colours),
        out_shape=[pltpu.VMEM((rows, LANES), jnp.int32)] * number + [pltpu.VMEM((EXTRA, block), jnp.int32)] * number,
        in_specs=[smem()] + [vmem()] * 6,
        out_specs=[vmem()] * (2 * number),
        compiler_params=params(8),
        name=f"plan_{number}",
    )(firsts, *near([zeros, own_rows, arrived, *first_known]))
    return dict(zip(colours, outs[:number])), dict(zip(colours, outs[number:]))


def add_older(now, newest, slots, plan, matrices, starts, outer, here, known, base):
    half, block = starts[0].shape
    operands = near([plan, *matrices, *starts, outer, here, *[known[c][side] for c, side in slots], *base])
    value, matrix = pltpu.VMEM((half, block), jnp.float32), pltpu.VMEM((block, block), jnp.bfloat16)
    return pl.pallas_call(
        functools.partial(older_kernel, newest, slots, len(base)),
        out_shape=[value, value, matrix, matrix],
        in_specs=[vmem()] * len(operands),
        out_specs=[vmem()] * 4,
        compiler_params=params(16),
        cost_estimate=pl.CostEstimate(
            flops=4 * block * block * LANES * (2 + len(slots)), bytes_accessed=24 * block * block, transcendentals=0
        ),
        name=f"older_{now}",
    )(*operands)


def run_relax(name, kernel, operands, half, block, outs):
    return pl.pallas_call(
        kernel,
        out_shape=[pltpu.VMEM((half, block), jnp.float32)] * outs,
        in_specs=[vmem()] * len(operands),
        out_specs=[vmem()] * outs,
        compiler_params=params(8),
        cost_estimate=pl.CostEstimate(
            flops=16 * block * block * LANES, bytes_accessed=16 * block * block, transcendentals=0
        ),
        name=name,
    )(*near(operands))


def per_device(residual, inv_diag, coupling_tiles, colour, tile_cols):
    axis = "rows"
    count = lax.axis_size(axis)
    groups = count // COLOURS
    me = lax.axis_index(axis)
    core = (me % 2).reshape(1)
    place = me % COLOURS
    group = me // COLOURS
    block, cols = residual.shape
    half = cols // 2
    tiles = jnp.transpose(coupling_tiles, (1, 0, 2))
    number = tiles.shape[0]

    def flip(value, bit):
        return lax.ppermute(value, axis, [(i, i ^ bit) for i in range(count)])

    def beside(value, ahead):
        pairs = []
        for i in range(count):
            step = COLOURS if (i // 2) % 2 == ahead else -COLOURS
            pairs.append((i, (i + step) % count))
        return lax.ppermute(value, axis, pairs)

    keep, send, own_rows = pl.pallas_call(
        first_kernel,
        out_shape=[pltpu.VMEM((half, block), jnp.float32)]
        + [pltpu.VMEM((half + EXTRA, block), jnp.float32), pltpu.VMEM((EXTRA, block), jnp.float32)],
        in_specs=[smem(), smem(), smem(), hbm(), hbm()],
        out_specs=[vmem()] * 3,
        scratch_shapes=[
            pltpu.VMEM((block, block), jnp.float32),
            pltpu.VMEM((block, cols), jnp.float32),
            pltpu.SemaphoreType.DMA((2,)),
        ],
        compiler_params=params(16),
        name="first",
    )(core, colour, tile_cols, *far([inv_diag, residual]))
    arrived = flip(send, 1)
    starts = [keep, arrived]

    late_tiles, _ = lax.optimization_barrier((tiles, arrived))
    sib_tiles, sib_inverse = flip(late_tiles, 1), flip(inv_diag, 1)

    own_wide, sib_wide = own_rows[:1], arrived[half : half + 1]
    candidate = jnp.where(own_wide == 0, keep, jnp.where(sib_wide == 0, arrived[:half], 0.0))
    wheel = lax.broadcasted_iota(jnp.int32, (EXTRA, block), 0).astype(jnp.float32)
    places = jnp.where(wheel == own_wide, place + 1, 0) + jnp.where(wheel == sib_wide, (place ^ 1) + 1, 0)
    places = places.astype(jnp.float32)
    sent = jnp.concatenate([candidate, places])
    swapped = flip(sent, 2)
    outer = beside(sent, 1)
    here = jnp.where((own_wide == 0) | (sib_wide == 0), candidate, swapped[:half])
    here = jnp.concatenate([here, places + swapped[half:]])
    known = {0: [beside(here, 0), outer, here]}
    toward = jnp.where(place < COLOURS // 2, -1, 1)
    firsts = jnp.stack([((group + step) % groups) * COLOURS for step in (toward, -toward, 0 * toward)]).astype(jnp.int32)
    far_tiles, far_inverse, _ = lax.optimization_barrier((tiles, inv_diag, here))
    *own_parts, zeros = parts(*far([far_tiles, far_inverse]), [here], "own_parts")
    *sib_parts, zeros = parts(sib_tiles, sib_inverse, [zeros], "sib_parts")
    matrices = [*own_parts, *sib_parts]
    facts = (firsts, own_rows, arrived, known[0])
    order = list(range(1, COLOURS)) + list(range(COLOURS - 2, -1, -1))
    plans, masks = make_plans(number, order[:1], *facts, zeros)
    newest = 0
    bases, included, finals = {}, {}, {}
    for step, now in enumerate(order):
        if step == 0:
            operands = [plans[now], *matrices, *starts, *known[newest]]
            kernel = functools.partial(first_relax_kernel, newest)
            candidate, bases[now] = run_relax(f"relax_{now}", kernel, operands, half, block, 2)
            included[now] = {(newest, -1, side) for side in range(SIDES)}
        else:
            operands = [plans[now], known[newest][INNER], *update]
            kernel = functools.partial(relax_kernel, newest)
            (candidate,) = run_relax(f"relax_{now}", kernel, operands, half, block, 1)
        finals[now] = candidate
        if step == len(order) - 1:
            break
        if step == 0:
            rest = list(range(COLOURS))
            for table, more in zip((plans, masks), make_plans(number, rest, *facts, candidate)):
                table.update(more)
        after = order[step + 1]
        swapped = flip(candidate, 2)
        outer = beside(candidate, 1)
        here = jnp.where(masks[now][:1] != 0, candidate, swapped)
        inner = beside(here, 0)
        have = included.get(after, set())
        slots, all_slots = [], {(now, step, OUTER), (now, step, HERE)}
        for c in sorted(known):
            for side in range(SIDES):
                if c not in (now, after):
                    all_slots.add((c, done_at(order, c, step), side))
                    if (c, done_at(order, c, step), side) not in have:
                        slots.append((c, side))
        base = [bases[after]] if after in bases else []
        partial, *update = add_older(after, now, slots, plans[after], matrices, starts, outer, here, known, base)
        bases[after], included[after] = partial, all_slots
        known[now] = [inner, outer, here]
        newest = now

    own_final, sib_final = finals[0], finals[0]
    for c in range(1, COLOURS):
        own_final = jnp.where(own_wide == c, finals[c], own_final)
        sib_final = jnp.where(sib_wide == c, finals[c], sib_final)
    mine, other = own_final, flip(sib_final, 1)
    return pl.pallas_call(
        last_kernel,
        out_shape=jax.ShapeDtypeStruct((block, cols), jnp.float32),
        in_specs=[smem(), vmem(), vmem()],
        out_specs=vmem(),
        compiler_params=params(16),
        name="last",
    )(core, *near([mine, other]))


def done_at(order, colour, step):
    return max([i for i in range(step) if order[i] == colour], default=-1)


def solution(mesh):
    in_specs = (P("rows", None), P("rows", None), P("rows", None, None), P("rows"), P("rows", None))
    out_specs = P("rows", None)
    return jax.shard_map(
        per_device, mesh=mesh, in_specs=in_specs, out_specs=out_specs, check_vma=False
    )
```
